32 devices in a mesh: cell: 16 (over z, x, core), mode: 2 (over y).
Axes of the slice: x: 2, y: 2, z: 4, core: 2. Of those that a mesh axis runs over, the one named last changes fastest.
Arguments:
- pod_modes: bfloat16 [3, 512, 4, 32, 128], P(None, 'mode', None, 'cell'), may hold values from -6 to 6
- slab_map: int32 [4, 32, 128], P(None, 'cell'), may hold values from 0 to 7
- slab_volume: float32 [8], replicated, may hold values from 0.25 to 4
- advect_index: int32 [8], replicated, may hold values from 0 to 511, as said below
- pair_adv: int32 [2048], replicated, may hold values from 0 to 7
- pair_mode: int32 [2048], replicated, may hold values from 0 to 511
- pair_amp: float32 [2048, 1024], replicated, may hold values from -0.2 to 0.2
Outputs:
- convective: float32 [512, 8, 512], P(('mode', 'cell'))
- response: float32 [512, 1024], P(('mode', 'cell'))
The draws below stay inside these ranges and needn't reach their ends.
Inputs may be any that keep to these rules, and one draw needn't show every extreme that they name: `advect_index`: 8 distinct mode indices.
All inputs are finite; a program needn't handle non-finite values.
Results may differ from the reference program's by a relative error of at most 0.0043.
Values may be sent and summed in bfloat16 or wider, within the bound.
No kernel may reach another device: no remote copies, remote signals or barrier semaphores. Data moves between devices by JAX's collectives and lax.ppermute only.
A program may use at most 128 MiB of HBM per device.

```python
import math
import jax
import jax.numpy as jnp
from jax import lax

M = 512
J = 8
P_SIZE = 2048
S = 1024
SLABS = 8
NX = 4
NZ = 128
NY = 32


def draw_advect_index(key, part):
    return jax.random.permutation(key, M)[:J].astype(jnp.int32)


def with_ends(result, own_key, low, top_value):
    extent = result.shape
    spot = [jax.random.randint(jax.random.fold_in(own_key, axis), (), 0, extent[axis]) for axis in range(len(extent))]
    result = result.at[tuple(spot)].set(low)
    longest = extent.index(max(extent))
    spot[longest] = (spot[longest] + 1) % extent[longest]
    return result.at[tuple(spot)].set(top_value)


def levels(own_key, dims, cuts, low, top_value):
    def one(axis_at, shards_of):
        draws = jax.random.uniform(jax.random.fold_in(jax.random.fold_in(own_key, 6), axis_at), (shards_of,), jnp.float32, low / len(cuts), top_value / len(cuts))
        return jnp.repeat(jnp.exp(draws), dims[axis_at] // shards_of).reshape((-1,) + (1,) * (len(dims) - axis_at - 1))

    gain = one(*cuts[0])
    for cut in cuts[1:]:
        gain = gain * one(*cut)
    return gain


def normal_values(stream_key, extent, scale, reach, pieces=(), kind=jnp.bfloat16):
    result = jax.random.normal(stream_key, extent, jnp.float32) * scale
    if len(pieces) > 0:
        result = levels(stream_key, extent, pieces, -0.22, 0.18) * result
    return jnp.clip(result, min=-reach, max=reach).astype(kind)


def setup_inputs(seed: int = 0) -> dict:
    key_list = jax.random.split(jax.random.key(seed), 8)
    pod_modes = normal_values(key_list[0], (3, M, NX, NY, NZ), 1.0, 6.0, ((1, 2), (3, 16)))
    slab_map = with_ends(jax.random.randint(key_list[1], (NX, NY, NZ), 0, SLABS), jax.random.fold_in(key_list[1], 1), 0, SLABS - 1).astype(jnp.int32)
    slab_volume = jnp.clip(jnp.exp(jax.random.uniform(key_list[2], (SLABS,), jnp.float32, math.log(0.25), math.log(4.0))), 0.25, 4.0)
    advect_index = draw_advect_index(jax.random.fold_in(key_list[7], 71), 0)
    pair_adv = with_ends(jax.random.randint(key_list[4], (P_SIZE,), 0, J), jax.random.fold_in(key_list[4], 1), 0, J - 1).astype(jnp.int32)
    pair_mode = with_ends(jax.random.randint(key_list[5], (P_SIZE,), 0, M), jax.random.fold_in(key_list[5], 1), 0, M - 1).astype(jnp.int32)
    pair_amp = normal_values(key_list[6], (P_SIZE, S), 0.03, 0.2, (), jnp.float32)
    return {"pod_modes": pod_modes, "slab_map": slab_map, "slab_volume": slab_volume, "advect_index": advect_index, "pair_adv": pair_adv, "pair_mode": pair_mode, "pair_amp": pair_amp}


def grads_of(field):
    along_x = 0.5 * (jnp.roll(field, -1, axis=2) - jnp.roll(field, 1, axis=2))
    padded = jnp.pad(field, ((0, 0), (0, 0), (0, 0), (1, 1), (0, 0)))
    along_y = 0.5 * (padded[:, :, :, 2:] - padded[:, :, :, :-2])
    along_z = 0.5 * (jnp.roll(field, -1, axis=4) - jnp.roll(field, 1, axis=4))
    return jnp.stack([along_x, along_y, along_z])


def reference(pod_modes, slab_map, slab_volume, advect_index, pair_adv, pair_mode, pair_amp):
    cell_total = NX * NY * NZ
    field = pod_modes.astype(jnp.float32)
    rounded = lax.optimization_barrier(grads_of(field).astype(jnp.bfloat16))
    grads = rounded.astype(jnp.float32).reshape(3, 3, M, cell_total)
    volume = slab_volume[slab_map].reshape(cell_total)
    flat_modes = pod_modes.astype(jnp.float32).reshape(3, M, cell_total)
    weighted = flat_modes[:, advect_index] * volume
    rows_per = 8

    def one_block(start_at):
        rows = lax.dynamic_slice_in_dim(flat_modes, start_at, rows_per, 1)
        left_factor = rows.transpose(1, 0, 2)[:, None, None, :, :] * weighted.transpose(1, 0, 2)[None, :, :, None, :]
        left_factor = lax.optimization_barrier(left_factor.astype(jnp.bfloat16)).astype(jnp.float32)
        return jnp.einsum("ijdcx,dckx->ijk", left_factor, grads)

    starts = (jnp.arange(M // rows_per) * rows_per).astype(jnp.int32)
    convective = lax.map(one_block, starts).reshape(M, J, M) * (cell_total ** -0.5)
    flat_rows = convective.reshape(M, J * M)
    pair_slot = pair_adv * M + pair_mode
    columns = jnp.take(flat_rows, pair_slot, axis=1)
    response = jnp.dot(columns, pair_amp, precision=lax.Precision.HIGHEST, preferred_element_type=jnp.float32)
    return convective, response
```

```python
import functools

import jax
import jax.numpy as jnp
from jax import lax
from jax.experimental import pallas as pl
from jax.experimental.pallas import tpu as pltpu
from jax.sharding import PartitionSpec as P

LANES = 128
F32 = jnp.float32
BF16 = jnp.bfloat16


def whole(memory_space=pltpu.VMEM):
    return pl.BlockSpec(memory_space=memory_space)


def params(mib):
    return pltpu.CompilerParams(vmem_limit_bytes=mib * 2**20)


def cost(flops, size):
    return pl.CostEstimate(flops=int(flops), bytes_accessed=int(size), transcendentals=0)


def pack_kernel(planes, rows_y, owners, chunks, base_ref, index_ref, pods_ref, *refs):
    row_refs, own_ref = refs[:rows_y], refs[rows_y]
    chunk_refs = refs[rows_y + 1 : rows_y + 1 + len(chunks)]
    chosen_ref, wide = refs[-2], refs[-1]
    modes, cells = pods_ref.shape[1], pods_ref.shape[2]
    wide[...] = pods_ref[0].astype(F32).reshape(modes * cells, LANES)
    per_owner = modes // owners
    for r in range(rows_y):
        for p in range(planes):
            value = wide[pl.ds(p * rows_y + r, modes, stride=cells), :]
            own = value.astype(BF16)
            at = (r * planes + p) * LANES
            row_refs[r][:, p * LANES : (p + 1) * LANES] = own
            own_ref[:, at : at + LANES] = own
            split = value.reshape(owners, per_owner, LANES)
            for ref, (first, count) in zip(chunk_refs, chunks):
                part = split[:, first : first + count].reshape(owners * count, LANES)
                ref[:, at : at + LANES] = part.astype(BF16)
    for j in range(chosen_ref.shape[1]):
        local = index_ref[j] - base_ref[0]
        inside = jnp.logical_and(local >= 0, local < modes)
        row = jnp.clip(local, 0, modes - 1) * cells
        found = wide[pl.ds(pl.multiple_of(row, cells), cells), :]
        chosen_ref[0, j] = jnp.where(inside, found, 0.0)


def pack(pods, advect_index, base, owners, chunks):
    comps, modes, planes, rows_y, width = pods.shape
    cells = planes * rows_y
    advect_count = advect_index.shape[0]
    flat = pods.reshape(comps, modes, cells, width)
    part = planes * width
    shapes = [((modes, comps * part), (modes, part))] * rows_y
    shapes += [((modes, comps * rows_y * part), (modes, rows_y * part))]
    for _, count in chunks:
        shapes += [((owners * count, comps * rows_y * part), (owners * count, rows_y * part))]
    out_shape = [jax.ShapeDtypeStruct(s, BF16) for s, _ in shapes]
    out_specs = [pl.BlockSpec(b, lambda c: (0, c)) for _, b in shapes]
    out_shape += [jax.ShapeDtypeStruct((comps, advect_count, cells, width), F32)]
    out_specs += [pl.BlockSpec((1, advect_count, cells, width), lambda c: (c, 0, 0, 0))]
    outs = pl.pallas_call(
        functools.partial(pack_kernel, planes, rows_y, owners, chunks),
        grid=(comps,),
        in_specs=[
            whole(pltpu.SMEM),
            whole(pltpu.SMEM),
            pl.BlockSpec((1, modes, cells, width), lambda c: (c, 0, 0, 0)),
        ],
        out_specs=out_specs,
        out_shape=out_shape,
        scratch_shapes=[pltpu.VMEM((modes * cells, width), F32)],
        compiler_params=params(24),
        cost_estimate=cost(0, 4 * pods.size * 2),
        name="pack",
    )(base.reshape(1), advect_index, flat)
    return outs[:rows_y], outs[rows_y], outs[rows_y + 1 : -1], outs[-1]


def advected_kernel(comps, planes, rows_y, volume_ref, map_ref, chosen_ref, *refs):
    row_refs, below_ref, above_ref = refs[:rows_y], refs[rows_y], refs[rows_y + 1]
    out_ref, weighted = refs[-2], refs[-1]
    advect_count = chosen_ref.shape[1]
    slabs = map_ref[...]
    volume = jnp.zeros(slabs.shape, F32)
    for level in range(volume_ref.shape[0]):
        volume = jnp.where(slabs == level, volume_ref[level], volume)
    for d in range(comps):
        for j in range(advect_count):
            weighted[d, j] = chosen_ref[d, j] * volume

    def rounded(x):
        return x.astype(BF16).astype(F32)

    def at(ref, c, p):
        lane = (c * planes + p % planes) * LANES
        return ref[:, lane : lane + LANES].astype(F32)

    for c in range(comps):
        for r in range(rows_y):
            for p in range(planes):
                u = at(row_refs[r], c, p)
                under = at(row_refs[r - 1] if r > 0 else below_ref, c, p)
                over = at(row_refs[r + 1] if r < rows_y - 1 else above_ref, c, p)
                grads = (
                    rounded(0.5 * (at(row_refs[r], c, p + 1) - at(row_refs[r], c, p - 1 + planes))),
                    rounded(0.5 * (over - under)),
                    rounded(0.5 * (pltpu.roll(u, LANES - 1, 1) - pltpu.roll(u, 1, 1))),
                )
                cell = p * rows_y + r
                lane = ((c * rows_y + r) * planes + p) * LANES
                for j in range(advect_count):
                    total = weighted[0, j, cell : cell + 1, :] * grads[0]
                    for d in range(1, comps):
                        total = total + weighted[d, j, cell : cell + 1, :] * grads[d]
                    out_ref[j, :, lane : lane + LANES] = total.astype(BF16)


def advected(rows, below, above, chosen, slab_map, slab_volume):
    comps, advect_count, cells, width = chosen.shape
    rows_y = len(rows)
    planes = cells // rows_y
    modes = rows[0].shape[0]
    tall = 32
    line = pl.BlockSpec((tall, rows[0].shape[1]), lambda b: (b, 0))
    depth = comps * cells * width
    return pl.pallas_call(
        functools.partial(advected_kernel, comps, planes, rows_y),
        grid=(modes // tall,),
        in_specs=[whole(pltpu.SMEM), whole(), whole()] + [line] * (rows_y + 2),
        out_specs=pl.BlockSpec((advect_count, tall, depth), lambda b: (0, b, 0)),
        out_shape=jax.ShapeDtypeStruct((advect_count, modes, depth), BF16),
        scratch_shapes=[pltpu.VMEM((comps, advect_count, cells, width), F32)],
        compiler_params=params(24),
        cost_estimate=cost(5 * advect_count * modes * depth, 2 * advect_count * modes * depth),
        name="advected",
    )(slab_volume, slab_map.reshape(cells, width), chosen, *rows, below, above)


def contract_kernel(left_ref, right_ref, out_ref):
    out_ref[...] = lax.dot_general(
        left_ref[...], right_ref[...], (((1,), (1,)), ((), ())), preferred_element_type=F32
    )


def contract(left, right):
    rows, depth = left.shape
    columns = right.shape[0]
    wide = min(columns, 256)
    return pl.pallas_call(
        contract_kernel,
        grid=(columns // wide,),
        in_specs=[whole(), pl.BlockSpec((wide, depth), lambda j: (j, 0))],
        out_specs=pl.BlockSpec((rows, wide), lambda j: (0, j)),
        out_shape=jax.ShapeDtypeStruct((rows, columns), F32),
        compiler_params=params(24),
        cost_estimate=cost(2 * rows * depth * columns, right.size * 2),
        name="contract",
    )(left, right)


def shifted(block, axis, distance, size, span):
    route = []
    for i in range(lax.axis_size(axis)):
        digit = i // span % size
        route.append((i, i + ((digit + distance) % size - digit) * span))
    return lax.ppermute(block, axis, route)


def stages(count):
    sizes = []
    while count % 4 == 0 and count > 4:
        sizes, count = sizes + [4], count // 4
    if count == 4:
        sizes, count = sizes + [2], 2
    return [count] + sizes[::-1] if count > 1 else sizes[::-1]


def owner_rows(partial):
    size = lax.axis_size("cell")
    own = lax.axis_index("cell")
    span = 1
    value = partial.reshape(size, -1, partial.shape[-1])
    for ways in stages(size):
        digit = own // span % ways
        value = value.reshape(-1, ways, *value.shape[1:])
        kept = lax.dynamic_index_in_dim(value, digit, 1, keepdims=False)
        for s in range(1, ways):
            sent = lax.dynamic_index_in_dim(value, (digit + s) % ways, 1, keepdims=False)
            kept = kept + shifted(sent.astype(BF16), "cell", s, ways, span).astype(F32)
        value = kept
        span *= ways
    return value[0]


def finish_kernel(blocks, advect_count, per_block, scale_factor, slot_ref, flat_ref, amp_ref, tensor_ref, out_ref, columns):
    rows = flat_ref.shape[0]
    step = pl.program_id(0)

    @pl.when(step == 0)
    def _():
        for b in range(blocks):
            for j in range(advect_count):
                at = (b * advect_count + j) * per_block
                tensor_ref[:, j, b * per_block : (b + 1) * per_block] = flat_ref[:, at : at + per_block] * scale_factor

    groups = flat_ref.shape[1] // LANES
    tall = columns.shape[1]
    for g in range(tall // LANES):
        slot = slot_ref[:, g * LANES : (g + 1) * LANES]
        lane = jnp.broadcast_to(slot % LANES, (rows, LANES))
        group = jnp.broadcast_to(slot // LANES, (rows, LANES))
        found = jnp.zeros((rows, LANES), F32)
        for s in range(groups):
            source = flat_ref[:, s * LANES : (s + 1) * LANES]
            found = jnp.where(group == s, jnp.take_along_axis(source, lane, axis=1), found)
        columns[:, g * LANES : (g + 1) * LANES] = found * scale_factor
    term = jnp.dot(columns[...], amp_ref[...], precision=lax.Precision.HIGHEST, preferred_element_type=F32)

    @pl.when(step == 0)
    def _():
        out_ref[...] = term

    @pl.when(step > 0)
    def _():
        out_ref[...] += term


def finish(flat, slot, amp, blocks, advect_count, per_block, scale_factor):
    rows = flat.shape[0]
    pairs, snaps = amp.shape
    tall = 512 if pairs % 512 == 0 else pairs
    return pl.pallas_call(
        functools.partial(finish_kernel, blocks, advect_count, per_block, scale_factor),
        grid=(pairs // tall,),
        in_specs=[
            pl.BlockSpec((1, tall), lambda i: (0, i)),
            whole(),
            pl.BlockSpec((tall, snaps), lambda i: (i, 0)),
        ],
        out_specs=[whole(), whole()],
        out_shape=[
            jax.ShapeDtypeStruct((rows, advect_count, blocks * per_block), F32),
            jax.ShapeDtypeStruct((rows, snaps), F32),
        ],
        scratch_shapes=[pltpu.VMEM((rows, tall), F32)],
        compiler_params=params(32),
        cost_estimate=cost(12 * rows * pairs * snaps, amp.size * 4),
        name="finish",
    )(slot.reshape(1, pairs), flat, amp)


def shards(pod_modes, slab_map, slab_volume, advect_index, pair_adv, pair_mode, pair_amp):
    comps, mode_block, planes, rows_y, width = pod_modes.shape
    mode_devs = lax.axis_size("mode")
    cell_devs = lax.axis_size("cell")
    advect_count = advect_index.shape[0]
    scale_factor = float(planes * rows_y * cell_devs * width) ** (-0.5)
    me = lax.axis_index("mode")
    rows_here = mode_block // cell_devs
    half = rows_here // 2
    chunks = ((0, half), (half, half)) if half % 8 == 0 else ()

    rows, own, parts, chosen = pack(pod_modes, advect_index, me * mode_block, cell_devs, chunks)
    parts = parts or [own]
    picked = chosen.astype(BF16)
    for s in range(1, mode_devs):
        chosen = chosen + shifted(picked, "mode", s, mode_devs, 1).astype(F32)
    arrived = [[shifted(part, "mode", s, mode_devs, 1) for part in parts] for s in range(1, mode_devs)]
    up = [(i, i + 1) for i in range(cell_devs - 1)]
    below = lax.ppermute(rows[-1], "cell", up)
    above = lax.ppermute(rows[0], "cell", [(j, i) for i, j in up])
    right = advected(rows, below, above, chosen, slab_map, slab_volume)
    right = right.reshape(-1, right.shape[-1])

    mine = owner_rows(contract(own, right))
    result = jnp.zeros((mode_devs,) + mine.shape, F32)
    result = lax.dynamic_update_index_in_dim(result, mine, me, 0)
    for s in range(1, mode_devs):
        block = jnp.concatenate([owner_rows(contract(part, right)) for part in arrived[s - 1]], axis=0)
        back = shifted(block, "mode", mode_devs - s, mode_devs, 1)
        result = lax.dynamic_update_index_in_dim(result, back, (me + s) % mode_devs, 0)
    flat = jnp.transpose(result, (1, 0, 2)).reshape(rows_here, -1)
    slot = (pair_mode // mode_block * advect_count + pair_adv) * mode_block + pair_mode % mode_block
    tensor, response = finish(flat, slot, pair_amp, mode_devs, advect_count, mode_block, scale_factor)
    return (tensor, response)


def solution(mesh):
    in_specs = (P(None, "mode", None, "cell", None), P(None, "cell", None), P(), P(), P(), P(), P())
    out_specs = (P(("mode", "cell"), None, None), P(("mode", "cell"), None))
    return jax.shard_map(shards, mesh=mesh, in_specs=in_specs, out_specs=out_specs, check_vma=False)
```

```python
import functools
import math

import jax
import jax.numpy as jnp
from jax import lax
from jax.experimental import pallas as pl
from jax.experimental.pallas import tpu as pltpu
from jax.sharding import PartitionSpec as P

LANES = 128
F32 = jnp.float32
BF16 = jnp.bfloat16


def whole(memory_space=pltpu.VMEM):
    return pl.BlockSpec(memory_space=memory_space)


def params(mib):
    return pltpu.CompilerParams(vmem_limit_bytes=mib * 2**20)


SHORT = pl.CostEstimate(flops=1, bytes_accessed=1, transcendentals=0)


def choose_kernel(index_ref, pods_ref, out_ref, held, sems):
    modes = pods_ref.shape[1]
    base = lax.axis_index("mode") * modes
    count = out_ref.shape[0]
    copies = []
    for j in range(count):
        local = jnp.clip(index_ref[j] - base, 0, modes - 1)
        copies.append(pltpu.make_async_copy(pods_ref.at[:, local], held.at[j], sems.at[j]))
        copies[-1].start()
    for j in range(count):
        copies[j].wait()
        local = index_ref[j] - base
        inside = jnp.logical_and(local >= 0, local < modes)
        out_ref[j] = jnp.where(inside, held[j].astype(F32), 0.0).astype(BF16)


def choose(flat, advect_index):
    comps, modes, cells, width = flat.shape
    shape = (advect_index.shape[0], comps, cells, width)
    return pl.pallas_call(
        choose_kernel,
        in_specs=[whole(pltpu.SMEM), whole(pltpu.HBM)],
        out_specs=whole(),
        out_shape=jax.ShapeDtypeStruct(shape, BF16),
        scratch_shapes=[pltpu.VMEM(shape, BF16), pltpu.SemaphoreType.DMA((shape[0],))],
        compiler_params=params(58),
        cost_estimate=SHORT,
        name="choose",
    )(advect_index, flat)


def pack_kernel(planes, rows_y, groups, apart, pods_ref, after_ref, *refs):
    comps, modes, cells, _ = pods_ref.shape
    part = planes * LANES
    outs, wide = refs[:-1], refs[-1]
    for g, group in enumerate(groups):
        for k, c in enumerate(group):
            wide[...] = pods_ref[c].astype(F32).reshape(modes * cells, LANES)
            for r in range(rows_y):
                for p in range(planes):
                    value = wide[pl.ds(p * rows_y + r, modes, stride=cells), :].astype(BF16)
                    ref = outs[g * rows_y + r] if apart else outs[g]
                    at = (k if apart else r * len(group) + k) * part + p * LANES
                    ref[:, at : at + LANES] = value


def pack(flat, after, planes, rows_y, groups, apart):
    comps, modes, cells, width = flat.shape
    part = planes * width
    shapes = []
    for group in groups:
        shapes += [(modes, len(group) * part)] * rows_y if apart else [(modes, len(group) * rows_y * part)]
    return pl.pallas_call(
        functools.partial(pack_kernel, planes, rows_y, groups, apart),
        in_specs=[whole(), whole(pl.ANY)],
        out_specs=[whole()] * len(shapes),
        out_shape=[jax.ShapeDtypeStruct(s, BF16) for s in shapes],
        scratch_shapes=[pltpu.VMEM((modes * cells, width), F32)],
        compiler_params=params(8),
        cost_estimate=SHORT,
        name="edges" if apart else "together",
    )(flat, after)


def advected_kernel(members, planes, rows_y, tall, volume_ref, map_ref, chosen_ref, back_ref, *refs):
    row_refs, below_ref, above_ref = refs[:rows_y], refs[rows_y], refs[rows_y + 1]
    out_ref, weighted = refs[-2], refs[-1]
    advect_count, comps = chosen_ref.shape[:2]
    modes = below_ref.shape[0]
    slabs = map_ref[...]
    volume = jnp.zeros(slabs.shape, F32)
    for level in range(volume_ref.shape[0]):
        volume = jnp.where(slabs == level, volume_ref[level], volume)
    for d in range(comps):
        for j in range(advect_count):
            chosen = chosen_ref[j, d].astype(F32)
            for s in range(back_ref.shape[0]):
                chosen = chosen + back_ref[s, j, d].astype(F32)
            weighted[d, j] = 0.5 * (chosen * volume)

    def rounded(x):
        return x.astype(BF16).astype(F32)

    @pl.loop(0, modes // tall)
    def _(b):
        here = pl.ds(pl.multiple_of(b * tall, tall), tall)

        def at(ref, k, p):
            lane = (k * planes + p) * LANES
            return ref[here, lane : lane + LANES].astype(F32)

        for k in range(members):
            lines = [[at(ref, k, p) for p in range(planes)] for ref in row_refs]
            for p in range(planes):
                column = [at(below_ref, k, p)] + [line[p] for line in lines] + [at(above_ref, k, p)]
                for r in range(rows_y):
                    u = lines[r][p]
                    grads = (
                        rounded(lines[r][(p + 1) % planes] - lines[r][(p - 1) % planes]),
                        rounded(column[r + 2] - column[r]),
                        rounded(pltpu.roll(u, LANES - 1, 1) - pltpu.roll(u, 1, 1)),
                    )
                    cell = p * rows_y + r
                    lane = ((r * members + k) * planes + p) * LANES
                    for j in range(advect_count):
                        total = weighted[0, j, cell : cell + 1, :] * grads[0]
                        for d in range(1, comps):
                            total = total + weighted[d, j, cell : cell + 1, :] * grads[d]
                        out_ref[j, here, lane : lane + LANES] = total.astype(BF16)


def advected(members, rows, below, above, chosen, back, slab_map, slab_volume):
    advect_count, comps, cells, width = chosen.shape
    rows_y = len(rows)
    planes = cells // rows_y
    modes = rows[0].shape[0]
    depth = members * cells * width
    return pl.pallas_call(
        functools.partial(advected_kernel, members, planes, rows_y, 16),
        in_specs=[whole(pltpu.SMEM)] + [whole()] * (rows_y + 5),
        out_specs=whole(),
        out_shape=jax.ShapeDtypeStruct((advect_count, modes, depth), BF16),
        scratch_shapes=[pltpu.VMEM((comps, advect_count, cells, width), F32)],
        compiler_params=params(8),
        cost_estimate=SHORT,
        name="advected",
    )(slab_volume, slab_map.reshape(cells, width), chosen, back, *rows, below, above)


def digits(number, sizes):
    ways, span = sizes[number], math.prod(sizes[:number])
    own = lax.axis_index("cell") // span % ways
    return [lax.rem(own + s, ways) for s in range(ways)]


def contract_kernel(sizes, groups, rows_y, wide, left_ref, *refs):
    outs = refs[len(groups) : -1]
    right_refs, scratch = refs[: len(groups)], refs[-1]
    columns = right_refs[0].shape[0]
    depth = left_ref.shape[1]
    comps = sum(len(group) for group in groups)
    part = depth // rows_y // comps
    pieces = []
    for group in groups:
        for r in range(rows_y):
            first = (r * comps + group[0]) * part
            pieces.append(left_ref[:, first : first + len(group) * part])
    left = jnp.concatenate(pieces, axis=1)
    places = digits(0, sizes)
    for n in range(columns // wide):
        here = slice(n * wide, (n + 1) * wide)
        right = jnp.concatenate([ref[here, :] for ref in right_refs], axis=1)
        value = lax.dot_general(left, right, (((1,), (1,)), ((), ())), preferred_element_type=F32)
        scratch[n % 2] = value.reshape(scratch.shape[1:])
        for q in range(outs[0].shape[0]):
            for out, place in zip(outs, places):
                out[q, :, here] = scratch[n % 2, q * sizes[0] + place].astype(out.dtype)


def contract(left, groups, right, sizes, rows_y):
    columns = right[0].shape[0]
    rows, depth = left.shape
    owners = math.prod(sizes)
    wide = min(columns, 256)
    shape = (owners // sizes[0], rows // owners, columns)
    return pl.pallas_call(
        functools.partial(contract_kernel, sizes, groups, rows_y, wide),
        in_specs=[whole()] * (1 + len(right)),
        out_specs=[whole()] * sizes[0],
        out_shape=[jax.ShapeDtypeStruct(shape, BF16 if s else F32) for s in range(sizes[0])],
        scratch_shapes=[pltpu.VMEM((2, owners, rows // owners, wide), F32)],
        compiler_params=params(8),
        cost_estimate=SHORT,
        name="contract",
    )(left, *right)


def fold_kernel(number, sizes, arrived, *refs):
    kept_ref, arrived_refs, outs = refs[0], refs[1 : 1 + arrived], refs[1 + arrived :]
    places = [0] if number == len(sizes) else digits(number, sizes)
    ways = len(places)
    for q in range(kept_ref.shape[0] // ways):
        for out, place in zip(outs, places):
            total = kept_ref[q * ways + place]
            for ref in arrived_refs:
                total = total + ref[q * ways + place].astype(F32)
            out[q] = total.astype(out.dtype)


def fold(kept, arrived, number, sizes):
    ways = 1 if number == len(sizes) else sizes[number]
    shape = (kept.shape[0] // ways, *kept.shape[1:])
    return pl.pallas_call(
        functools.partial(fold_kernel, number, sizes, len(arrived)),
        in_specs=[whole()] * (1 + len(arrived)),
        out_specs=[whole()] * ways,
        out_shape=[jax.ShapeDtypeStruct(shape, BF16 if s else F32) for s in range(ways)],
        compiler_params=params(8),
        cost_estimate=SHORT,
        name="fold",
    )(kept, *arrived)


def shifted(block, axis, distance, size, span):
    route = []
    for i in range(lax.axis_size(axis)):
        digit = i // span % size
        route.append((i, i + ((digit + distance) % size - digit) * span))
    return lax.ppermute(block, axis, route)


def stages(count):
    sizes = []
    while count % 4 == 0 and count > 4:
        sizes, count = sizes + [4], count // 4
    if count == 4:
        sizes, count = sizes + [2], 2
    return [count] + sizes[::-1] if count > 1 else sizes[::-1]


def stage(parts, number, sizes):
    span = math.prod(sizes[:number])
    arrived = [shifted(part, "cell", s + 1, sizes[number], span) for s, part in enumerate(parts[1:])]
    return fold(parts[0], arrived, number + 1, sizes)


def finish_kernel(advect_count, per_block, scale_factor, me_ref, slot_ref, *refs):
    *part_refs, amp_ref, tensor_ref, out_ref, flat, both, amps, sems = refs
    blocks, rows = flat.shape[0], flat.shape[1]
    steps, tall, _ = amps.shape
    copies = []
    for i in range(steps):
        copies.append(pltpu.make_async_copy(amp_ref.at[pl.ds(i * tall, tall)], amps.at[i], sems.at[i]))
        copies[-1].start()
    for s, ref in enumerate(part_refs):
        flat[s] = ref[...] * scale_factor
    for b in range(blocks):
        for j in range(advect_count):
            at = slice(j * per_block, (j + 1) * per_block)
            value = flat[0, :, at]
            for s in range(1, blocks):
                value = jnp.where((me_ref[0] + s) % blocks == b, flat[s, :, at], value)
            tensor_ref[:, j, b * per_block : (b + 1) * per_block] = value

    groups = flat.shape[2] // LANES
    for g in range(both.shape[1] // LANES):
        here = slice(g * LANES, (g + 1) * LANES)
        slot = slot_ref[:, here]
        lane = jnp.broadcast_to(slot % LANES, (rows, LANES))
        group = jnp.broadcast_to(slot // LANES, (rows, LANES))
        found = jnp.zeros((rows, LANES), F32)
        for b in range(blocks):
            for s in range(groups):
                source = flat[b, :, s * LANES : (s + 1) * LANES]
                taken = jnp.take_along_axis(source, lane, axis=1)
                found = jnp.where(group == b * groups + s, taken, found)
        high = found.astype(BF16).astype(F32)
        both[:rows, here] = high
        both[rows:, here] = found - high
    total = jnp.zeros(out_ref.shape, F32)
    for i in range(steps):
        copies[i].wait()
        columns = both[:, i * tall : (i + 1) * tall].astype(BF16)
        amp = amps[i]
        high = amp.astype(BF16)
        low = (amp - high.astype(F32)).astype(BF16)
        term = jnp.dot(columns, high, preferred_element_type=F32)
        small = jnp.dot(columns[:rows], low, preferred_element_type=F32)
        total = total + (term[:rows] + (term[rows:] + small))
    out_ref[...] = total


def finish(me, slot, parts, amp, advect_count, scale_factor):
    pairs, snaps = amp.shape
    tall = 512 if pairs % 512 == 0 else pairs
    rows, columns = parts[0].shape
    blocks = len(parts)
    per_block = columns // advect_count
    return pl.pallas_call(
        functools.partial(finish_kernel, advect_count, per_block, scale_factor),
        in_specs=[whole(pltpu.SMEM)] + [whole()] * (1 + blocks) + [whole(pltpu.HBM)],
        out_specs=[whole(), whole()],
        out_shape=[
            jax.ShapeDtypeStruct((rows, advect_count, blocks * per_block), F32),
            jax.ShapeDtypeStruct((rows, snaps), F32),
        ],
        scratch_shapes=[
            pltpu.VMEM((blocks, rows, columns), F32),
            pltpu.VMEM((2 * rows, pairs), F32),
            pltpu.VMEM((pairs // tall, tall, snaps), F32),
            pltpu.SemaphoreType.DMA((pairs // tall,)),
        ],
        compiler_params=params(58),
        cost_estimate=SHORT,
        name="finish",
    )(me.reshape(1), slot.reshape(1, pairs), *parts, amp)


def shards(pod_modes, slab_map, slab_volume, advect_index, pair_adv, pair_mode, pair_amp):
    comps, mode_block, planes, rows_y, width = pod_modes.shape
    mode_devs = lax.axis_size("mode")
    cell_devs = lax.axis_size("cell")
    advect_count = advect_index.shape[0]
    scale_factor = float(planes * rows_y * cell_devs * width) ** (-0.5)
    me = lax.axis_index("mode")
    rows_here = mode_block // cell_devs

    flat = pod_modes.reshape(comps, mode_block, planes * rows_y, width)
    chosen = choose(flat, advect_index)
    everything = (tuple(range(comps)),)
    groups = (tuple(range(comps - 1)), (comps - 1,))
    (own,) = pack(flat, chosen, planes, rows_y, everything, False)
    back = jnp.stack([shifted(chosen, "mode", s, mode_devs, 1) for s in range(1, mode_devs)])
    own, back = lax.optimization_barrier((own, back))
    arrived = [shifted(own, "mode", s, mode_devs, 1) for s in range(1, mode_devs)]
    up = [(i, i + 1) for i in range(cell_devs - 1)]
    down = [(j, i) for i, j in up]
    before, halos = own, []
    for group in groups:
        lines = pack(flat, before, planes, rows_y, (group,), True)
        halos.append((lines, lax.ppermute(lines[-1], "cell", up), lax.ppermute(lines[0], "cell", down)))
        before = lines[0]
    right = []
    for group, (lines, below, above) in zip(groups, halos):
        if right:
            right[-1], below, above = lax.optimization_barrier((right[-1], below, above))
        block = advected(len(group), lines, below, above, chosen, back, slab_map, slab_volume)
        right.append(block.reshape(-1, block.shape[-1]))

    sizes = stages(cell_devs)
    early = min(2, len(sizes))

    def summed(parts, first, last):
        for number in range(first, last):
            parts = stage(parts, number, sizes)
        return list(parts)

    mine = summed(contract(own, groups, right, sizes, rows_y), 0, early)
    mine[0], *arrived = lax.optimization_barrier((mine[0], *arrived))
    result = []
    for s in range(1, mode_devs):
        block = summed(contract(arrived[s - 1], groups, right, sizes, rows_y), 0, early)
        if s == 1:
            mine = summed(mine, early, len(sizes))
            mine[0], block[0] = lax.optimization_barrier((mine[0], block[0]))
            result.append(mine[0][0])
        block = summed(block, early, len(sizes))[0][0]
        result.append(shifted(block, "mode", mode_devs - s, mode_devs, 1))
    block_of = (pair_mode // mode_block - me) % mode_devs
    slot = (block_of * advect_count + pair_adv) * mode_block + pair_mode % mode_block
    tensor, response = finish(me, slot, result, pair_amp, advect_count, scale_factor)
    return (tensor, response)


def solution(mesh):
    in_specs = (P(None, "mode", None, "cell", None), P(None, "cell", None), P(), P(), P(), P(), P())
    out_specs = (P(("mode", "cell"), None, None), P(("mode", "cell"), None))
    return jax.shard_map(shards, mesh=mesh, in_specs=in_specs, out_specs=out_specs, check_vma=False)
```

```python
import functools
import math

import jax
import jax.numpy as jnp
from jax import lax
from jax.experimental import pallas as pl
from jax.experimental.pallas import tpu as pltpu
from jax.sharding import PartitionSpec as P

LANES = 128
F32 = jnp.float32
BF16 = jnp.bfloat16


def whole(memory_space=pltpu.VMEM):
    return pl.BlockSpec(memory_space=memory_space)


def params(mib):
    return pltpu.CompilerParams(vmem_limit_bytes=mib * 2**20)


SHORT = pl.CostEstimate(flops=1, bytes_accessed=1, transcendentals=0)


def lead_places(comps, advect_count, lanes):
    pairs = -(-advect_count // 2)
    spot = [divmod(c * pairs + j, lanes // LANES) for c in range(comps) for j in range(pairs)]
    return pairs, [(row * 16, lane * LANES) for row, lane in spot]


def lead_kernel(planes, rows_y, first, count, advect_count, *refs):
    index_ref, pods_ref, wide = refs[0], refs[1], refs[-1]
    ahead = refs[-2].shape == pods_ref.shape
    out_ref = refs[-3] if ahead else refs[-2]
    if ahead:
        refs[-2][...] = pods_ref[...]
    comps, modes, cells, _ = pods_ref.shape
    base = lax.axis_index("mode") * modes
    extra = out_ref.shape[0] - count
    pairs, places = lead_places(comps, advect_count, out_ref.shape[1])
    if extra:
        out_ref[:extra, :] = jnp.zeros((extra, out_ref.shape[1]), BF16)
    for c in range(comps):
        wide[...] = pods_ref[c].astype(F32).reshape(modes * cells, LANES)
        for r in range(rows_y):
            for p in range(planes):
                value = wide[pl.ds(first * cells + p * rows_y + r, count, stride=cells), :]
                at = ((r * comps + c) * planes + p) * LANES
                out_ref[extra:, at : at + LANES] = value.astype(BF16)
        for pair in range(pairs if extra else 0):
            blocks = []
            for j in (2 * pair, 2 * pair + 1):
                local = index_ref[min(j, advect_count - 1)] - base
                inside = jnp.logical_and(local >= 0, local < modes)
                row = pl.multiple_of(jnp.clip(local, 0, modes - 1) * cells, cells)
                blocks.append(jnp.where(inside, wide[pl.ds(row, cells), :], 0.0))
            row, lane = places[c * pairs + pair]
            out_ref[row : row + 2 * cells, lane : lane + LANES] = jnp.concatenate(blocks, axis=0).astype(BF16)


def lead(flat, advect_index, after, planes, rows_y, first, count, ahead):
    comps, modes, cells, width = flat.shape
    lanes = comps * cells * width
    extra = 0
    if ahead:
        _, places = lead_places(comps, advect_index.shape[0], lanes)
        extra = places[-1][0] + 16
    return pl.pallas_call(
        functools.partial(lead_kernel, planes, rows_y, first, count, advect_index.shape[0]),
        in_specs=[whole(pltpu.SMEM), whole()] + [whole(pl.ANY)] * len(after),
        out_specs=[whole()] * (1 + ahead),
        out_shape=[jax.ShapeDtypeStruct((extra + count, lanes), BF16)]
        + [jax.ShapeDtypeStruct(flat.shape, BF16)] * ahead,
        scratch_shapes=[pltpu.VMEM((modes * cells, width), F32)],
        compiler_params=params(8),
        cost_estimate=SHORT,
        name="lead",
    )(advect_index, flat, *after)


def edge_kernel(planes, rows_y, r, pods_ref, after_ref, out_ref, wide):
    comps, modes, cells, _ = pods_ref.shape
    for c in range(comps):
        wide[...] = pods_ref[c].astype(F32).reshape(modes * cells, LANES)
        for p in range(planes):
            value = wide[pl.ds(p * rows_y + r, modes, stride=cells), :]
            at = (c * planes + p) * LANES
            out_ref[:, at : at + LANES] = value.astype(BF16)


def edge(flat, after, planes, rows_y, r):
    comps, modes, cells, width = flat.shape
    return pl.pallas_call(
        functools.partial(edge_kernel, planes, rows_y, r),
        in_specs=[whole(), whole(pl.ANY)],
        out_specs=whole(),
        out_shape=jax.ShapeDtypeStruct((modes, comps * planes * width), BF16),
        scratch_shapes=[pltpu.VMEM((modes * cells, width), F32)],
        compiler_params=params(8),
        cost_estimate=SHORT,
        name="edge",
    )(flat, after)


def weight_kernel(volume_ref, map_ref, after_ref, out_ref):
    slabs = map_ref[...]
    weight = jnp.zeros(slabs.shape, F32)
    for level in range(volume_ref.shape[0]):
        weight = jnp.where(slabs == level, volume_ref[level], weight)
    out_ref[...] = weight


def weights(slab_map, slab_volume, after):
    planes, rows_y, width = slab_map.shape
    shape = (planes * rows_y, width)
    return pl.pallas_call(
        weight_kernel,
        in_specs=[whole(pltpu.SMEM), whole(), whole(pl.ANY)],
        out_specs=whole(),
        out_shape=jax.ShapeDtypeStruct(shape, F32),
        compiler_params=params(8),
        cost_estimate=SHORT,
        name="weights",
    )(slab_volume, slab_map.reshape(shape), after)


def advected_kernel(comps, planes, rows_y, r, tall, weight_ref, here_ref, under_ref, over_ref, *refs):
    lead_refs, out_ref, weighted = refs[:-2], refs[-2], refs[-1]
    advect_count = out_ref.shape[0]
    modes = here_ref.shape[0]
    cells = planes * rows_y
    weight = weight_ref[...]
    pairs, places = lead_places(comps, advect_count, lead_refs[0].shape[1])
    for d in range(comps):
        for pair in range(pairs):
            row, lane = places[d * pairs + pair]
            both = jnp.zeros((2 * cells, LANES), F32)
            for ref in lead_refs:
                both = both + ref[row : row + 2 * cells, lane : lane + LANES].astype(F32)
            for k in range(min(2, advect_count - 2 * pair)):
                weighted[d, 2 * pair + k] = 0.5 * (both[k * cells : (k + 1) * cells] * weight)

    def rounded(x):
        return x.astype(BF16).astype(F32)

    @pl.loop(0, modes // tall)
    def _(b):
        here = pl.ds(pl.multiple_of(b * tall, tall), tall)

        def at(ref, k, p):
            lane = (k * planes + p) * LANES
            return ref[here, lane : lane + LANES].astype(F32)

        for k in range(comps):
            line = [at(here_ref, k, p) for p in range(planes)]
            for p in range(planes):
                grads = (
                    rounded(line[(p + 1) % planes] - line[(p - 1) % planes]),
                    rounded(at(over_ref, k, p) - at(under_ref, k, p)),
                    rounded(pltpu.roll(line[p], LANES - 1, 1) - pltpu.roll(line[p], 1, 1)),
                )
                cell = p * rows_y + r
                lane = (k * planes + p) * LANES
                for j in range(advect_count):
                    total = weighted[0, j, cell : cell + 1, :] * grads[0]
                    for d in range(1, comps):
                        total = total + weighted[d, j, cell : cell + 1, :] * grads[d]
                    out_ref[j, here, lane : lane + LANES] = total.astype(BF16)


def advected(leads, here, under, over, weight, rows_y, r, advect_count):
    cells, width = weight.shape
    planes = cells // rows_y
    modes, depth = here.shape
    comps = depth // (planes * width)
    return pl.pallas_call(
        functools.partial(advected_kernel, comps, planes, rows_y, r, 32),
        in_specs=[whole()] * (len(leads) + 4),
        out_specs=whole(),
        out_shape=jax.ShapeDtypeStruct((advect_count, modes, depth), BF16),
        scratch_shapes=[pltpu.VMEM((comps, advect_count, cells, width), F32)],
        compiler_params=params(8),
        cost_estimate=SHORT,
        name="advected",
    )(weight, here, under, over, *leads)


def digits(number, sizes):
    ways, span = sizes[number], math.prod(sizes[:number])
    own = lax.axis_index("cell") // span % ways
    return [lax.rem(own + s, ways) for s in range(ways)]


def contract_kernel(sizes, wide, rows_y, ahead_ref, rest_ref, *refs):
    right_refs, outs, scratch = refs[:rows_y], refs[rows_y:-1], refs[-1]
    columns = right_refs[0].shape[0]
    extra = ahead_ref.shape[0] - rest_ref.shape[0]
    left = jnp.concatenate([ahead_ref[extra:, :], rest_ref[...]], axis=0)
    places = digits(0, sizes)
    for n in range(columns // wide):
        here = slice(n * wide, (n + 1) * wide)
        right = jnp.concatenate([ref[here, :] for ref in right_refs], axis=1)
        value = lax.dot_general(left, right, (((1,), (1,)), ((), ())), preferred_element_type=F32)
        scratch[n % 2] = value.reshape(scratch.shape[1:])
        for q in range(outs[0].shape[0]):
            for out, place in zip(outs, places):
                out[q, :, here] = scratch[n % 2, q * sizes[0] + place].astype(out.dtype)


def contract(left, right, sizes):
    columns = right[0].shape[0]
    rows = 2 * left[1].shape[0]
    owners = math.prod(sizes)
    wide = min(columns, 256)
    shape = (owners // sizes[0], rows // owners, columns)
    return pl.pallas_call(
        functools.partial(contract_kernel, sizes, wide, len(right)),
        in_specs=[whole()] * (2 + len(right)),
        out_specs=[whole()] * sizes[0],
        out_shape=[jax.ShapeDtypeStruct(shape, BF16 if s else F32) for s in range(sizes[0])],
        scratch_shapes=[pltpu.VMEM((2, owners, rows // owners, wide), F32)],
        compiler_params=params(8),
        cost_estimate=SHORT,
        name="contract",
    )(*left, *right)


def fold_kernel(number, sizes, arrived, *refs):
    kept_ref, arrived_refs, outs = refs[0], refs[1 : 1 + arrived], refs[1 + arrived :]
    places = [0] if number == len(sizes) else digits(number, sizes)
    ways = len(places)
    for q in range(kept_ref.shape[0] // ways):
        for out, place in zip(outs, places):
            total = kept_ref[q * ways + place]
            for ref in arrived_refs:
                total = total + ref[q * ways + place].astype(F32)
            out[q] = total.astype(out.dtype)


def fold(kept, arrived, number, sizes):
    ways = 1 if number == len(sizes) else sizes[number]
    shape = (kept.shape[0] // ways, *kept.shape[1:])
    return pl.pallas_call(
        functools.partial(fold_kernel, number, sizes, len(arrived)),
        in_specs=[whole()] * (1 + len(arrived)),
        out_specs=[whole()] * ways,
        out_shape=[jax.ShapeDtypeStruct(shape, BF16 if s else F32) for s in range(ways)],
        compiler_params=params(8),
        cost_estimate=SHORT,
        name="fold",
    )(kept, *arrived)


def shifted(block, axis, distance, size, span):
    route = []
    for i in range(lax.axis_size(axis)):
        digit = i // span % size
        route.append((i, i + ((digit + distance) % size - digit) * span))
    return lax.ppermute(block, axis, route)


def stages(count):
    sizes = []
    while count % 4 == 0 and count > 4:
        sizes, count = sizes + [4], count // 4
    if count == 4:
        sizes, count = sizes + [2], 2
    return [count] + sizes[::-1] if count > 1 else sizes[::-1]


def stage(parts, number, sizes):
    span = math.prod(sizes[:number])
    arrived = [shifted(part, "cell", s + 1, sizes[number], span) for s, part in enumerate(parts[1:])]
    return fold(parts[0], arrived, number + 1, sizes)


def finish_kernel(advect_count, per_block, scale_factor, adv_ref, mode_ref, *refs):
    *part_refs, amp_ref, tensor_ref, out_ref, flat, both, amps, sems = refs
    blocks, rows = flat.shape[0], flat.shape[1]
    steps, tall, _ = amps.shape
    me = lax.axis_index("mode")
    copies = []
    for i in range(steps):
        copies.append(pltpu.make_async_copy(amp_ref.at[pl.ds(i * tall, tall)], amps.at[i], sems.at[i]))
        copies[-1].start()
    for s, ref in enumerate(part_refs):
        flat[s] = ref[...] * scale_factor
    for b in range(blocks):
        for j in range(advect_count):
            at = slice(j * per_block, (j + 1) * per_block)
            value = flat[0, :, at]
            for s in range(1, blocks):
                value = jnp.where(lax.rem(me + s, blocks) == b, flat[s, :, at], value)
            tensor_ref[:, j, b * per_block : (b + 1) * per_block] = value

    groups = flat.shape[2] // LANES
    for g in range(both.shape[1] // LANES):
        here = slice(g * LANES, (g + 1) * LANES)
        mode = mode_ref[:, here]
        part = lax.rem(mode // per_block - me + blocks, blocks)
        slot = (part * advect_count + adv_ref[:, here]) * per_block + lax.rem(mode, per_block)
        lane = jnp.broadcast_to(lax.rem(slot, LANES), (rows, LANES))
        group = jnp.broadcast_to(slot // LANES, (rows, LANES))
        found = jnp.zeros((rows, LANES), F32)
        for b in range(blocks):
            for s in range(groups):
                source = flat[b, :, s * LANES : (s + 1) * LANES]
                taken = jnp.take_along_axis(source, lane, axis=1)
                found = jnp.where(group == b * groups + s, taken, found)
        high = found.astype(BF16).astype(F32)
        both[:rows, here] = high
        both[rows:, here] = found - high
    total = jnp.zeros(out_ref.shape, F32)
    for i in range(steps):
        copies[i].wait()
        columns = both[:, i * tall : (i + 1) * tall].astype(BF16)
        amp = amps[i]
        high = amp.astype(BF16)
        low = (amp - high.astype(F32)).astype(BF16)
        term = jnp.dot(columns, high, preferred_element_type=F32)
        small = jnp.dot(columns[:rows], low, preferred_element_type=F32)
        total = total + (term[:rows] + (term[rows:] + small))
    out_ref[...] = total


def finish(pair_adv, pair_mode, parts, amp, advect_count, scale_factor):
    pairs, snaps = amp.shape
    tall = 512 if pairs % 512 == 0 else pairs
    rows, columns = parts[0].shape
    blocks = len(parts)
    per_block = columns // advect_count
    return pl.pallas_call(
        functools.partial(finish_kernel, advect_count, per_block, scale_factor),
        in_specs=[whole()] * (2 + blocks) + [whole(pltpu.HBM)],
        out_specs=[whole(), whole()],
        out_shape=[
            jax.ShapeDtypeStruct((rows, advect_count, blocks * per_block), F32),
            jax.ShapeDtypeStruct((rows, snaps), F32),
        ],
        scratch_shapes=[
            pltpu.VMEM((blocks, rows, columns), F32),
            pltpu.VMEM((2 * rows, pairs), F32),
            pltpu.VMEM((pairs // tall, tall, snaps), F32),
            pltpu.SemaphoreType.DMA((pairs // tall,)),
        ],
        compiler_params=params(52),
        cost_estimate=SHORT,
        name="finish",
    )(pair_adv.reshape(1, pairs), pair_mode.reshape(1, pairs), *parts, amp)


def shards(pod_modes, slab_map, slab_volume, advect_index, pair_adv, pair_mode, pair_amp):
    comps, mode_block, planes, rows_y, width = pod_modes.shape
    mode_devs = lax.axis_size("mode")
    cell_devs = lax.axis_size("cell")
    advect_count = advect_index.shape[0]
    scale_factor = float(planes * rows_y * cell_devs * width) ** (-0.5)
    me = lax.axis_index("mode")
    rows_here = mode_block // cell_devs

    flat = pod_modes.reshape(comps, mode_block, planes * rows_y, width)
    half = mode_block // 2
    first, held = lead(flat, advect_index, (), planes, rows_y, 0, half, True)
    own = [first]
    rows, before = {}, own[0]
    for r in [rows_y - 1, *range(rows_y - 1)]:
        rows[r] = edge(held, before, planes, rows_y, r)
        before = rows[r]
    own += lead(held, advect_index, (before,), planes, rows_y, half, mode_block - half, False)
    weight = weights(slab_map, slab_volume, own[1])
    arrived = [[shifted(block, "mode", s, mode_devs, 1) for block in own] for s in range(1, mode_devs)]
    up = [(i, i + 1) for i in range(cell_devs - 1)]
    rows[-1] = lax.ppermute(rows[rows_y - 1], "cell", up)
    rows[rows_y] = lax.ppermute(rows[0], "cell", [(j, i) for i, j in up])
    leads = [own[0]] + [block[0] for block in arrived]
    right = []
    for r in range(rows_y):
        if right:
            right[-1], rows[r + 1] = lax.optimization_barrier((right[-1], rows[r + 1]))
        block = advected(leads, rows[r], rows[r - 1], rows[r + 1], weight, rows_y, r, advect_count)
        right.append(block.reshape(-1, block.shape[-1]))

    sizes = stages(cell_devs)
    early = min(1, len(sizes))

    def summed(parts, first, last):
        for number in range(first, min(last, len(sizes))):
            parts = stage(parts, number, sizes)
        return list(parts)

    mine = summed(contract(own, right, sizes), 0, early)
    mine[0], arrived = lax.optimization_barrier((mine[0], arrived))
    mine = summed(mine, early, early + 1)
    result = []
    for s in range(1, mode_devs):
        block = contract(arrived[s - 1], right, sizes)
        if s == 1:
            mine, block = lax.optimization_barrier((mine, block))
        block = summed(block, 0, early + 1)
        if s == 1:
            mine = summed(mine, early + 1, len(sizes))
            mine, block = lax.optimization_barrier((mine, block))
            result.append(mine[0][0])
        block = summed(block, early + 1, len(sizes))[0][0]
        result.append(shifted(block, "mode", mode_devs - s, mode_devs, 1))
    tensor, response = finish(pair_adv, pair_mode, result, pair_amp, advect_count, scale_factor)
    return (tensor, response)


def solution(mesh):
    in_specs = (P(None, "mode", None, "cell", None), P(None, "cell", None), P(), P(), P(), P(), P())
    out_specs = (P(("mode", "cell"), None, None), P(("mode", "cell"), None))
    return jax.shard_map(shards, mesh=mesh, in_specs=in_specs, out_specs=out_specs, check_vma=False)
```

```python
import functools
import math

import jax
import jax.numpy as jnp
from jax import lax
from jax.experimental import pallas as pl
from jax.experimental.pallas import tpu as pltpu
from jax.sharding import PartitionSpec as P

LANES = 128
F32 = jnp.float32
BF16 = jnp.bfloat16


def whole(memory_space=pltpu.VMEM):
    return pl.BlockSpec(memory_space=memory_space)


def params(mib):
    return pltpu.CompilerParams(vmem_limit_bytes=mib * 2**20)


SHORT = pl.CostEstimate(flops=1, bytes_accessed=1, transcendentals=0)


def lead_places(comps, advect_count, lanes):
    pairs = -(-advect_count // 2)
    spot = [divmod(c * pairs + j, lanes // LANES) for c in range(comps) for j in range(pairs)]
    return pairs, [(row * 16, lane * LANES) for row, lane in spot]


def lead_kernel(planes, rows_y, first, count, advect_count, *refs):
    index_ref, pods_ref, wide = refs[0], refs[1], refs[-1]
    ahead = refs[-2].shape == pods_ref.shape
    out_ref = refs[-3] if ahead else refs[-2]
    if ahead:
        refs[-2][...] = pods_ref[...]
    comps, modes, cells, _ = pods_ref.shape
    base = lax.axis_index("mode") * modes
    extra = out_ref.shape[0] - count
    pairs, places = lead_places(comps, advect_count, out_ref.shape[1])
    if extra:
        out_ref[:extra, :] = jnp.zeros((extra, out_ref.shape[1]), BF16)
    for c in range(comps):
        wide[...] = pods_ref[c].astype(F32).reshape(modes * cells, LANES)
        for r in range(rows_y):
            for p in range(planes):
                value = wide[pl.ds(first * cells + p * rows_y + r, count, stride=cells), :]
                at = ((r * comps + c) * planes + p) * LANES
                out_ref[extra:, at : at + LANES] = value.astype(BF16)
        for pair in range(pairs if extra else 0):
            blocks = []
            for j in (2 * pair, 2 * pair + 1):
                local = index_ref[min(j, advect_count - 1)] - base
                inside = jnp.logical_and(local >= 0, local < modes)
                row = pl.multiple_of(jnp.clip(local, 0, modes - 1) * cells, cells)
                blocks.append(jnp.where(inside, wide[pl.ds(row, cells), :], 0.0))
            row, lane = places[c * pairs + pair]
            out_ref[row : row + 2 * cells, lane : lane + LANES] = jnp.concatenate(blocks, axis=0).astype(BF16)


def lead(flat, advect_index, after, planes, rows_y, first, count, ahead):
    comps, modes, cells, width = flat.shape
    lanes = comps * cells * width
    extra = 0
    if ahead:
        _, places = lead_places(comps, advect_index.shape[0], lanes)
        extra = places[-1][0] + 16
    return pl.pallas_call(
        functools.partial(lead_kernel, planes, rows_y, first, count, advect_index.shape[0]),
        in_specs=[whole(pltpu.SMEM), whole()] + [whole(pl.ANY)] * len(after),
        out_specs=[whole()] * (1 + ahead),
        out_shape=[jax.ShapeDtypeStruct((extra + count, lanes), BF16)]
        + [jax.ShapeDtypeStruct(flat.shape, BF16)] * ahead,
        scratch_shapes=[pltpu.VMEM((modes * cells, width), F32)],
        compiler_params=params(8),
        cost_estimate=SHORT,
        name="lead",
    )(advect_index, flat, *after)


def edge_kernel(planes, rows_y, r, pods_ref, after_ref, out_ref, wide):
    comps, modes, cells, _ = pods_ref.shape
    for c in range(comps):
        wide[...] = pods_ref[c].astype(F32).reshape(modes * cells, LANES)
        for p in range(planes):
            value = wide[pl.ds(p * rows_y + r, modes, stride=cells), :]
            at = (c * planes + p) * LANES
            out_ref[:, at : at + LANES] = value.astype(BF16)


def edge(flat, after, planes, rows_y, r):
    comps, modes, cells, width = flat.shape
    return pl.pallas_call(
        functools.partial(edge_kernel, planes, rows_y, r),
        in_specs=[whole(), whole(pl.ANY)],
        out_specs=whole(),
        out_shape=jax.ShapeDtypeStruct((modes, comps * planes * width), BF16),
        scratch_shapes=[pltpu.VMEM((modes * cells, width), F32)],
        compiler_params=params(8),
        cost_estimate=SHORT,
        name="edge",
    )(flat, after)


def weight_kernel(volume_ref, map_ref, after_ref, out_ref):
    slabs = map_ref[...]
    weight = jnp.zeros(slabs.shape, F32)
    for level in range(volume_ref.shape[0]):
        weight = jnp.where(slabs == level, volume_ref[level], weight)
    out_ref[...] = weight


def weights(slab_map, slab_volume, after):
    planes, rows_y, width = slab_map.shape
    shape = (planes * rows_y, width)
    return pl.pallas_call(
        weight_kernel,
        in_specs=[whole(pltpu.SMEM), whole(), whole(pl.ANY)],
        out_specs=whole(),
        out_shape=jax.ShapeDtypeStruct(shape, F32),
        compiler_params=params(8),
        cost_estimate=SHORT,
        name="weights",
    )(slab_volume, slab_map.reshape(shape), after)


def advected_kernel(comps, planes, rows_y, r, tall, weight_ref, here_ref, under_ref, over_ref, *refs):
    lead_refs, out_ref, weighted = refs[:-2], refs[-2], refs[-1]
    advect_count = out_ref.shape[0]
    modes = here_ref.shape[0]
    cells = planes * rows_y
    weight = weight_ref[...]
    pairs, places = lead_places(comps, advect_count, lead_refs[0].shape[1])
    for d in range(comps):
        for pair in range(pairs):
            row, lane = places[d * pairs + pair]
            both = jnp.zeros((2 * cells, LANES), F32)
            for ref in lead_refs:
                both = both + ref[row : row + 2 * cells, lane : lane + LANES].astype(F32)
            for k in range(min(2, advect_count - 2 * pair)):
                weighted[d, 2 * pair + k] = 0.5 * (both[k * cells : (k + 1) * cells] * weight)

    def rounded(x):
        return x.astype(BF16).astype(F32)

    @pl.loop(0, modes // tall)
    def _(b):
        here = pl.ds(pl.multiple_of(b * tall, tall), tall)

        def at(ref, k, p):
            lane = (k * planes + p) * LANES
            return ref[here, lane : lane + LANES].astype(F32)

        for k in range(comps):
            line = [at(here_ref, k, p) for p in range(planes)]
            for p in range(planes):
                grads = (
                    rounded(line[(p + 1) % planes] - line[(p - 1) % planes]),
                    rounded(at(over_ref, k, p) - at(under_ref, k, p)),
                    rounded(pltpu.roll(line[p], LANES - 1, 1) - pltpu.roll(line[p], 1, 1)),
                )
                cell = p * rows_y + r
                lane = (k * planes + p) * LANES
                for j in range(advect_count):
                    total = weighted[0, j, cell : cell + 1, :] * grads[0]
                    for d in range(1, comps):
                        total = total + weighted[d, j, cell : cell + 1, :] * grads[d]
                    out_ref[j, here, lane : lane + LANES] = total.astype(BF16)


def advected(leads, here, under, over, weight, rows_y, r, advect_count):
    cells, width = weight.shape
    planes = cells // rows_y
    modes, depth = here.shape
    comps = depth // (planes * width)
    return pl.pallas_call(
        functools.partial(advected_kernel, comps, planes, rows_y, r, 32),
        in_specs=[whole()] * (len(leads) + 4),
        out_specs=whole(),
        out_shape=jax.ShapeDtypeStruct((advect_count, modes, depth), BF16),
        scratch_shapes=[pltpu.VMEM((comps, advect_count, cells, width), F32)],
        compiler_params=params(8),
        cost_estimate=SHORT,
        name="advected",
    )(weight, here, under, over, *leads)


def digits(number, sizes):
    ways, span = sizes[number], math.prod(sizes[:number])
    own = lax.axis_index("cell") // span % ways
    return [lax.rem(own + s, ways) for s in range(ways)]


def contract_kernel(sizes, wide, rows_y, ahead_ref, rest_ref, *refs):
    right_refs, outs, scratch = refs[:rows_y], refs[rows_y:-1], refs[-1]
    columns = right_refs[0].shape[0]
    extra = ahead_ref.shape[0] - rest_ref.shape[0]
    left = jnp.concatenate([ahead_ref[extra:, :], rest_ref[...]], axis=0)
    places = digits(0, sizes)
    for n in range(columns // wide):
        here = slice(n * wide, (n + 1) * wide)
        right = jnp.concatenate([ref[here, :] for ref in right_refs], axis=1)
        value = lax.dot_general(left, right, (((1,), (1,)), ((), ())), preferred_element_type=F32)
        scratch[n % 2] = value.reshape(scratch.shape[1:])
        for q in range(outs[0].shape[0]):
            for out, place in zip(outs, places):
                out[q, :, here] = scratch[n % 2, q * sizes[0] + place].astype(out.dtype)


def contract(left, right, sizes):
    columns = right[0].shape[0]
    rows = 2 * left[1].shape[0]
    owners = math.prod(sizes)
    wide = min(columns, 256)
    shape = (owners // sizes[0], rows // owners, columns)
    return pl.pallas_call(
        functools.partial(contract_kernel, sizes, wide, len(right)),
        in_specs=[whole()] * (2 + len(right)),
        out_specs=[whole()] * sizes[0],
        out_shape=[jax.ShapeDtypeStruct(shape, BF16 if s else F32) for s in range(sizes[0])],
        scratch_shapes=[pltpu.VMEM((2, owners, rows // owners, wide), F32)],
        compiler_params=params(8),
        cost_estimate=SHORT,
        name="contract",
    )(*left, *right)


def fold_kernel(number, sizes, arrived, *refs):
    kept_ref, arrived_refs, outs = refs[0], refs[1 : 1 + arrived], refs[1 + arrived :]
    places = [0] if number == len(sizes) else digits(number, sizes)
    ways = len(places)
    for q in range(kept_ref.shape[0] // ways):
        for out, place in zip(outs, places):
            total = kept_ref[q * ways + place]
            for ref in arrived_refs:
                total = total + ref[q * ways + place].astype(F32)
            out[q] = total.astype(out.dtype)


def fold(kept, arrived, number, sizes, all_leave=False):
    ways = 1 if number == len(sizes) else sizes[number]
    shape = (kept.shape[0] // ways, *kept.shape[1:])
    return pl.pallas_call(
        functools.partial(fold_kernel, number, sizes, len(arrived)),
        in_specs=[whole()] * (1 + len(arrived)),
        out_specs=[whole()] * ways,
        out_shape=[jax.ShapeDtypeStruct(shape, BF16 if s or all_leave else F32) for s in range(ways)],
        compiler_params=params(8),
        cost_estimate=SHORT,
        name="fold",
    )(kept, *arrived)


def shifted(block, axis, distance, size, span, turn=0):
    reach, turns = lax.axis_size(axis), lax.axis_size("mode") if turn else 1
    route = []
    for i in range(reach):
        digit = i // span % size
        to = i + ((digit + distance) % size - digit) * span
        route += [(i * turns + m, to * turns + (m + turn) % turns) for m in range(turns)]
    return lax.ppermute(block, (axis, "mode") if turn else axis, route)


def stages(count):
    sizes = []
    while count % 4 == 0 and count > 4:
        sizes, count = sizes + [4], count // 4
    if count == 4:
        sizes, count = sizes + [2], 2
    return [count] + sizes[::-1] if count > 1 else sizes[::-1]


def stage(parts, number, sizes, all_leave=False):
    span = math.prod(sizes[:number])
    arrived = [shifted(part, "cell", s + 1, sizes[number], span) for s, part in enumerate(parts[1:])]
    return fold(parts[0], arrived, number + 1, sizes, all_leave)


def prepare_kernel(amp_ref, high_ref, low_ref, amps, sems):
    steps, tall, _ = amps.shape
    copies = []
    for i in range(steps):
        copies.append(pltpu.make_async_copy(amp_ref.at[pl.ds(i * tall, tall)], amps.at[i], sems.at[i]))
        copies[-1].start()
    for i in range(steps):
        copies[i].wait()
        amp = amps[i]
        high = amp.astype(BF16)
        high_ref[i * tall : (i + 1) * tall, :] = high
        low_ref[i * tall : (i + 1) * tall, :] = (amp - high.astype(F32)).astype(BF16)


def prepare(amp):
    pairs, snaps = amp.shape
    tall = 256 if pairs % 256 == 0 else pairs
    return pl.pallas_call(
        prepare_kernel,
        in_specs=[whole(pltpu.HBM)],
        out_specs=[whole()] * 2,
        out_shape=[jax.ShapeDtypeStruct(amp.shape, BF16)] * 2,
        scratch_shapes=[
            pltpu.VMEM((pairs // tall, tall, snaps), F32),
            pltpu.SemaphoreType.DMA((pairs // tall,)),
        ],
        compiler_params=params(24),
        cost_estimate=pl.CostEstimate(flops=4 * amp.size, bytes_accessed=8 * amp.size, transcendentals=0),
        name="prepare",
    )(amp)


def finish_kernel(advect_count, per_block, scale_factor, counts, adv_ref, mode_ref, *refs):
    *part_refs, high_ref, low_ref, tensor_ref, out_ref, flat = refs
    blocks, rows = flat.shape[0], flat.shape[1]
    me = lax.axis_index("mode")
    tall = 512 if high_ref.shape[0] % 512 == 0 else high_ref.shape[0]
    steps = high_ref.shape[0] // tall
    terms = iter(part_refs)
    for s, count in enumerate(counts):
        total = next(terms)[0].astype(F32)
        for _ in range(count - 1):
            total = total + next(terms)[0].astype(F32)
        flat[s] = total * scale_factor
    for b in range(blocks):
        for j in range(advect_count):
            at = slice(j * per_block, (j + 1) * per_block)
            value = flat[0, :, at]
            for s in range(1, blocks):
                value = jnp.where(lax.rem(me + s, blocks) == b, flat[s, :, at], value)
            tensor_ref[:, j, b * per_block : (b + 1) * per_block] = value

    groups = flat.shape[2] // LANES

    def columns(i):
        high, low = [], []
        for g in range(i * tall // LANES, (i + 1) * tall // LANES):
            here = slice(g * LANES, (g + 1) * LANES)
            mode = mode_ref[:, here]
            part = lax.rem(mode // per_block - me + blocks, blocks)
            slot = (part * advect_count + adv_ref[:, here]) * per_block + lax.rem(mode, per_block)
            lane = jnp.broadcast_to(lax.rem(slot, LANES), (rows, LANES))
            group = jnp.broadcast_to(slot // LANES, (rows, LANES))
            found = jnp.zeros((rows, LANES), F32)
            for b in range(blocks):
                for s in range(groups):
                    source = flat[b, :, s * LANES : (s + 1) * LANES]
                    taken = jnp.take_along_axis(source, lane, axis=1)
                    found = jnp.where(group == b * groups + s, taken, found)
            high.append(found.astype(BF16).astype(F32))
            low.append(found - high[-1])
        both = [jnp.concatenate(high, axis=1), jnp.concatenate(low, axis=1)]
        return jnp.concatenate(both, axis=0).astype(BF16)

    total = jnp.zeros(out_ref.shape, F32)
    now = columns(0)
    for i in range(steps):
        here = slice(i * tall, (i + 1) * tall)
        term = jnp.dot(now, high_ref[here, :], preferred_element_type=F32)
        small = jnp.dot(now[:rows], low_ref[here, :], preferred_element_type=F32)
        if i < steps - 1:
            now = columns(i + 1)
        total = total + (term[:rows] + (term[rows:] + small))
    out_ref[...] = total


def finish(pair_adv, pair_mode, parts, high, low, advect_count, scale_factor):
    pairs, snaps = high.shape
    _, rows, columns = parts[0][0].shape
    blocks = len(parts)
    counts = [len(part) for part in parts]
    terms = [term for part in parts for term in part]
    per_block = columns // advect_count
    return pl.pallas_call(
        functools.partial(finish_kernel, advect_count, per_block, scale_factor, counts),
        in_specs=[whole()] * (4 + len(terms)),
        out_specs=[whole(), whole()],
        out_shape=[
            jax.ShapeDtypeStruct((rows, advect_count, blocks * per_block), F32),
            jax.ShapeDtypeStruct((rows, snaps), F32),
        ],
        scratch_shapes=[pltpu.VMEM((blocks, rows, columns), F32)],
        compiler_params=params(8),
        cost_estimate=SHORT,
        name="finish",
    )(pair_adv.reshape(1, pairs), pair_mode.reshape(1, pairs), *terms, high, low)


def shards(pod_modes, slab_map, slab_volume, advect_index, pair_adv, pair_mode, pair_amp):
    comps, mode_block, planes, rows_y, width = pod_modes.shape
    mode_devs = lax.axis_size("mode")
    cell_devs = lax.axis_size("cell")
    advect_count = advect_index.shape[0]
    scale_factor = float(planes * rows_y * cell_devs * width) ** (-0.5)
    me = lax.axis_index("mode")
    rows_here = mode_block // cell_devs

    flat = pod_modes.reshape(comps, mode_block, planes * rows_y, width)
    half = mode_block // 2
    first, held = lead(flat, advect_index, (), planes, rows_y, 0, half, True)
    own = [first]
    rows, before = {}, own[0]
    for r in [rows_y - 1, *range(rows_y - 1)]:
        rows[r] = edge(held, before, planes, rows_y, r)
        before = rows[r]
    own += lead(held, advect_index, (before,), planes, rows_y, half, mode_block - half, False)
    weight = weights(slab_map, slab_volume, own[1])
    arrived = [[shifted(block, "mode", s, mode_devs, 1) for block in own] for s in range(1, mode_devs)]
    up = [(i, i + 1) for i in range(cell_devs - 1)]
    rows[-1] = lax.ppermute(rows[rows_y - 1], "cell", up)
    rows[rows_y] = lax.ppermute(rows[0], "cell", [(j, i) for i, j in up])
    leads = [own[0]] + [block[0] for block in arrived]
    right = []
    for r in range(rows_y):
        if right:
            right[-1], rows[r + 1] = lax.optimization_barrier((right[-1], rows[r + 1]))
        block = advected(leads, rows[r], rows[r - 1], rows[r + 1], weight, rows_y, r, advect_count)
        right.append(block.reshape(-1, block.shape[-1]))

    sizes = stages(cell_devs)
    early, last = min(1, len(sizes)), len(sizes) - 1

    def summed(parts, first, end, sizes):
        for number in range(first, min(end, len(sizes))):
            parts = stage(parts, number, sizes)
        return list(parts)

    pairwise = sizes[:-1] + [2, 2] if sizes[-1] == 4 else sizes
    mine = summed(contract(own, right, pairwise), 0, early, pairwise)
    mine[0], arrived = lax.optimization_barrier((mine[0], arrived))
    mine = summed(mine, early, early + 1, pairwise)
    result = []
    for s in range(1, mode_devs):
        block = contract(arrived[s - 1], right, sizes)
        if s == 1:
            mine, block = lax.optimization_barrier((mine, block))
        block = stage(summed(block, 0, last - 1, sizes), last - 1, sizes, True)
        if s == 1:
            mine = summed(mine, early + 1, early + 2, pairwise)
            mine, block, pair_amp = lax.optimization_barrier((mine, block, pair_amp))
            result.append(summed(mine, early + 2, len(pairwise), pairwise))
        span = math.prod(sizes[:last])
        result.append([shifted(b, "cell", n, sizes[last], span, mode_devs - s) for n, b in enumerate(block)])
    high, low = prepare(pair_amp)
    tensor, response = finish(pair_adv, pair_mode, result, high, low, advect_count, scale_factor)
    return (tensor, response)


def solution(mesh):
    in_specs = (P(None, "mode", None, "cell", None), P(None, "cell", None), P(), P(), P(), P(), P())
    out_specs = (P(("mode", "cell"), None, None), P(("mode", "cell"), None))
    return jax.shard_map(shards, mesh=mesh, in_specs=in_specs, out_specs=out_specs, check_vma=False)
```

```python
import functools
import math

import jax
import jax.numpy as jnp
from jax import lax
from jax.experimental import pallas as pl
from jax.experimental.pallas import tpu as pltpu
from jax.sharding import PartitionSpec as P

LANES = 128
F32 = jnp.float32
BF16 = jnp.bfloat16


def whole(memory_space=pltpu.VMEM):
    return pl.BlockSpec(memory_space=memory_space)


def params(mib):
    return pltpu.CompilerParams(vmem_limit_bytes=mib * 2**20)


SHORT = pl.CostEstimate(flops=1, bytes_accessed=1, transcendentals=0)


def lead_places(comps, advect_count, lanes):
    pairs = -(-advect_count // 2)
    spot = [divmod(c * pairs + j, lanes // LANES) for c in range(comps) for j in range(pairs)]
    return pairs, [(row * 16, lane * LANES) for row, lane in spot]


def lead_kernel(planes, rows_y, first, count, advect_count, *refs):
    index_ref, pods_ref, wide = refs[0], refs[1], refs[-1]
    ahead = refs[-2].shape == pods_ref.shape
    out_ref = refs[-3] if ahead else refs[-2]
    if ahead:
        refs[-2][...] = pods_ref[...]
    comps, modes, cells, _ = pods_ref.shape
    base = lax.axis_index("mode") * modes
    extra = out_ref.shape[0] - count
    pairs, places = lead_places(comps, advect_count, out_ref.shape[1])
    if extra:
        out_ref[:extra, :] = jnp.zeros((extra, out_ref.shape[1]), BF16)
    for c in range(comps):
        wide[...] = pods_ref[c].astype(F32).reshape(modes * cells, LANES)
        for r in range(rows_y):
            for p in range(planes):
                value = wide[pl.ds(first * cells + p * rows_y + r, count, stride=cells), :]
                at = ((r * comps + c) * planes + p) * LANES
                out_ref[extra:, at : at + LANES] = value.astype(BF16)
        for pair in range(pairs if extra else 0):
            blocks = []
            for j in (2 * pair, 2 * pair + 1):
                local = index_ref[min(j, advect_count - 1)] - base
                inside = jnp.logical_and(local >= 0, local < modes)
                row = pl.multiple_of(jnp.clip(local, 0, modes - 1) * cells, cells)
                blocks.append(jnp.where(inside, wide[pl.ds(row, cells), :], 0.0))
            row, lane = places[c * pairs + pair]
            out_ref[row : row + 2 * cells, lane : lane + LANES] = jnp.concatenate(blocks, axis=0).astype(BF16)


def lead(flat, advect_index, after, planes, rows_y, first, count, ahead):
    comps, modes, cells, width = flat.shape
    lanes = comps * cells * width
    extra = 0
    if ahead:
        _, places = lead_places(comps, advect_index.shape[0], lanes)
        extra = places[-1][0] + 16
    return pl.pallas_call(
        functools.partial(lead_kernel, planes, rows_y, first, count, advect_index.shape[0]),
        in_specs=[whole(pltpu.SMEM), whole()] + [whole(pl.ANY)] * len(after),
        out_specs=[whole()] * (1 + ahead),
        out_shape=[jax.ShapeDtypeStruct((extra + count, lanes), BF16)]
        + [jax.ShapeDtypeStruct(flat.shape, BF16)] * ahead,
        scratch_shapes=[pltpu.VMEM((modes * cells, width), F32)],
        compiler_params=params(8),
        cost_estimate=SHORT,
        name="lead",
    )(advect_index, flat, *after)


def edge_kernel(planes, rows_y, r, pods_ref, after_ref, out_ref, wide):
    comps, modes, cells, _ = pods_ref.shape
    for c in range(comps):
        wide[...] = pods_ref[c].astype(F32).reshape(modes * cells, LANES)
        for p in range(planes):
            value = wide[pl.ds(p * rows_y + r, modes, stride=cells), :]
            at = (c * planes + p) * LANES
            out_ref[:, at : at + LANES] = value.astype(BF16)


def edge(flat, after, planes, rows_y, r):
    comps, modes, cells, width = flat.shape
    return pl.pallas_call(
        functools.partial(edge_kernel, planes, rows_y, r),
        in_specs=[whole(), whole(pl.ANY)],
        out_specs=whole(),
        out_shape=jax.ShapeDtypeStruct((modes, comps * planes * width), BF16),
        scratch_shapes=[pltpu.VMEM((modes * cells, width), F32)],
        compiler_params=params(8),
        cost_estimate=SHORT,
        name="edge",
    )(flat, after)


def weight_kernel(volume_ref, map_ref, after_ref, out_ref):
    slabs = map_ref[...]
    weight = jnp.zeros(slabs.shape, F32)
    for level in range(volume_ref.shape[0]):
        weight = jnp.where(slabs == level, volume_ref[level], weight)
    out_ref[...] = weight


def weights(slab_map, slab_volume, after):
    planes, rows_y, width = slab_map.shape
    shape = (planes * rows_y, width)
    return pl.pallas_call(
        weight_kernel,
        in_specs=[whole(pltpu.SMEM), whole(), whole(pl.ANY)],
        out_specs=whole(),
        out_shape=jax.ShapeDtypeStruct(shape, F32),
        compiler_params=params(8),
        cost_estimate=SHORT,
        name="weights",
    )(slab_volume, slab_map.reshape(shape), after)


def advected_kernel(comps, planes, rows_y, r, tall, weight_ref, here_ref, under_ref, over_ref, *refs):
    lead_refs, out_ref, weighted = refs[:-2], refs[-2], refs[-1]
    advect_count = out_ref.shape[0]
    modes = here_ref.shape[0]
    cells = planes * rows_y
    weight = weight_ref[...]
    pairs, places = lead_places(comps, advect_count, lead_refs[0].shape[1])
    for d in range(comps):
        for pair in range(pairs):
            row, lane = places[d * pairs + pair]
            both = jnp.zeros((2 * cells, LANES), F32)
            for ref in lead_refs:
                both = both + ref[row : row + 2 * cells, lane : lane + LANES].astype(F32)
            for k in range(min(2, advect_count - 2 * pair)):
                weighted[d, 2 * pair + k] = 0.5 * (both[k * cells : (k + 1) * cells] * weight)

    def difference(x, y):
        return (x - y).astype(F32)

    @pl.loop(0, modes // tall)
    def _(b):
        here = pl.ds(pl.multiple_of(b * tall, tall), tall)

        def at(ref, k, p):
            lane = (k * planes + p) * LANES
            return ref[here, lane : lane + LANES]

        for k in range(comps):
            line = [at(here_ref, k, p) for p in range(planes)]
            for p in range(planes):
                grads = (
                    difference(line[(p + 1) % planes], line[(p - 1) % planes]),
                    difference(at(over_ref, k, p), at(under_ref, k, p)),
                    difference(pltpu.roll(line[p], LANES - 1, 1), pltpu.roll(line[p], 1, 1)),
                )
                cell = p * rows_y + r
                lane = (k * planes + p) * LANES
                for j in range(advect_count):
                    total = weighted[0, j, cell : cell + 1, :] * grads[0]
                    for d in range(1, comps):
                        total = total + weighted[d, j, cell : cell + 1, :] * grads[d]
                    out_ref[j, here, lane : lane + LANES] = total.astype(BF16)


def advected(leads, here, under, over, weight, rows_y, r, advect_count):
    cells, width = weight.shape
    planes = cells // rows_y
    modes, depth = here.shape
    comps = depth // (planes * width)
    return pl.pallas_call(
        functools.partial(advected_kernel, comps, planes, rows_y, r, 32),
        in_specs=[whole()] * (len(leads) + 4),
        out_specs=whole(),
        out_shape=jax.ShapeDtypeStruct((advect_count, modes, depth), BF16),
        scratch_shapes=[pltpu.VMEM((comps, advect_count, cells, width), F32)],
        compiler_params=params(8),
        cost_estimate=SHORT,
        name="advected",
    )(weight, here, under, over, *leads)


def digits(number, sizes):
    ways, span = sizes[number], math.prod(sizes[:number])
    own = lax.axis_index("cell") // span % ways
    return [lax.rem(own + s, ways) for s in range(ways)]


def contract_kernel(sizes, wide, rows_y, ahead_ref, rest_ref, *refs):
    right_refs, outs, scratch = refs[:rows_y], refs[rows_y:-1], refs[-1]
    columns = right_refs[0].shape[0]
    extra = ahead_ref.shape[0] - rest_ref.shape[0]
    left = jnp.concatenate([ahead_ref[extra:, :], rest_ref[...]], axis=0)
    places = digits(0, sizes)
    for n in range(columns // wide):
        here = slice(n * wide, (n + 1) * wide)
        right = jnp.concatenate([ref[here, :] for ref in right_refs], axis=1)
        value = lax.dot_general(left, right, (((1,), (1,)), ((), ())), preferred_element_type=F32)
        scratch[n % 2] = value.reshape(scratch.shape[1:])
        for q in range(outs[0].shape[0]):
            for out, place in zip(outs, places):
                out[q, :, here] = scratch[n % 2, q * sizes[0] + place].astype(out.dtype)


def contract(left, right, sizes):
    columns = right[0].shape[0]
    rows = 2 * left[1].shape[0]
    owners = math.prod(sizes)
    wide = min(columns, 256)
    shape = (owners // sizes[0], rows // owners, columns)
    return pl.pallas_call(
        functools.partial(contract_kernel, sizes, wide, len(right)),
        in_specs=[whole()] * (2 + len(right)),
        out_specs=[whole()] * sizes[0],
        out_shape=[jax.ShapeDtypeStruct(shape, BF16 if s else F32) for s in range(sizes[0])],
        scratch_shapes=[pltpu.VMEM((2, owners, rows // owners, wide), F32)],
        compiler_params=params(8),
        cost_estimate=SHORT,
        name="contract",
    )(*left, *right)


def fold_kernel(number, sizes, arrived, *refs):
    kept_ref, arrived_refs, outs = refs[0], refs[1 : 1 + arrived], refs[1 + arrived :]
    places = [0] if number == len(sizes) else digits(number, sizes)
    ways = len(places)
    for q in range(kept_ref.shape[0] // ways):
        for out, place in zip(outs, places):
            total = kept_ref[q * ways + place]
            for ref in arrived_refs:
                total = total + ref[q * ways + place].astype(F32)
            out[q] = total.astype(out.dtype)


def fold(kept, arrived, number, sizes, all_leave=False):
    ways = 1 if number == len(sizes) else sizes[number]
    shape = (kept.shape[0] // ways, *kept.shape[1:])
    return pl.pallas_call(
        functools.partial(fold_kernel, number, sizes, len(arrived)),
        in_specs=[whole()] * (1 + len(arrived)),
        out_specs=[whole()] * ways,
        out_shape=[jax.ShapeDtypeStruct(shape, BF16 if s or all_leave else F32) for s in range(ways)],
        compiler_params=params(8),
        cost_estimate=SHORT,
        name="fold",
    )(kept, *arrived)


def shifted(block, axis, distance, size, span, turn=0):
    reach, turns = lax.axis_size(axis), lax.axis_size("mode") if turn else 1
    route = []
    for i in range(reach):
        digit = i // span % size
        to = i + ((digit + distance) % size - digit) * span
        route += [(i * turns + m, to * turns + (m + turn) % turns) for m in range(turns)]
    return lax.ppermute(block, (axis, "mode") if turn else axis, route)


def stages(count):
    sizes = []
    while count % 4 == 0 and count > 4:
        sizes, count = sizes + [4], count // 4
    if count == 4:
        sizes, count = sizes + [2], 2
    return [count] + sizes[::-1] if count > 1 else sizes[::-1]


def stage(parts, number, sizes, all_leave=False):
    span = math.prod(sizes[:number])
    arrived = [shifted(part, "cell", s + 1, sizes[number], span) for s, part in enumerate(parts[1:])]
    return fold(parts[0], arrived, number + 1, sizes, all_leave)


def prepare_kernel(amp_ref, high_ref, low_ref, amps, sems):
    steps, tall, _ = amps.shape
    copies = []
    for i in range(steps):
        copies.append(pltpu.make_async_copy(amp_ref.at[pl.ds(i * tall, tall)], amps.at[i], sems.at[i]))
        copies[-1].start()
    for i in range(steps):
        copies[i].wait()
        amp = amps[i]
        high = amp.astype(BF16)
        high_ref[i * tall : (i + 1) * tall, :] = high
        low_ref[i * tall : (i + 1) * tall, :] = (amp - high.astype(F32)).astype(BF16)


def prepare(amp):
    pairs, snaps = amp.shape
    tall = 256 if pairs % 256 == 0 else pairs
    return pl.pallas_call(
        prepare_kernel,
        in_specs=[whole(pltpu.HBM)],
        out_specs=[whole()] * 2,
        out_shape=[jax.ShapeDtypeStruct(amp.shape, BF16)] * 2,
        scratch_shapes=[
            pltpu.VMEM((pairs // tall, tall, snaps), F32),
            pltpu.SemaphoreType.DMA((pairs // tall,)),
        ],
        compiler_params=params(24),
        cost_estimate=pl.CostEstimate(flops=4 * amp.size, bytes_accessed=8 * amp.size, transcendentals=0),
        name="prepare",
    )(amp)


def finish_kernel(advect_count, per_block, scale_factor, counts, adv_ref, mode_ref, *refs):
    *part_refs, high_ref, low_ref, tensor_ref, out_ref, flat = refs
    blocks, rows = flat.shape[0], flat.shape[1]
    me = lax.axis_index("mode")
    tall = 512 if high_ref.shape[0] % 512 == 0 else high_ref.shape[0]
    steps = high_ref.shape[0] // tall
    terms = iter(part_refs)
    for s, count in enumerate(counts):
        total = next(terms)[0].astype(F32)
        for _ in range(count - 1):
            total = total + next(terms)[0].astype(F32)
        flat[s] = total * scale_factor
    for b in range(blocks):
        for j in range(advect_count):
            at = slice(j * per_block, (j + 1) * per_block)
            value = flat[0, :, at]
            for s in range(1, blocks):
                value = jnp.where(lax.rem(me + s, blocks) == b, flat[s, :, at], value)
            tensor_ref[:, j, b * per_block : (b + 1) * per_block] = value

    groups = flat.shape[2] // LANES

    def columns(i):
        high, low = [], []
        for g in range(i * tall // LANES, (i + 1) * tall // LANES):
            here = slice(g * LANES, (g + 1) * LANES)
            mode = mode_ref[:, here]
            part = lax.rem(mode // per_block - me + blocks, blocks)
            slot = (part * advect_count + adv_ref[:, here]) * per_block + lax.rem(mode, per_block)
            lane = jnp.broadcast_to(lax.rem(slot, LANES), (rows, LANES))
            group = jnp.broadcast_to(slot // LANES, (rows, LANES))
            found = jnp.zeros((rows, LANES), F32)
            for b in range(blocks):
                for s in range(groups):
                    source = flat[b, :, s * LANES : (s + 1) * LANES]
                    taken = jnp.take_along_axis(source, lane, axis=1)
                    found = jnp.where(group == b * groups + s, taken, found)
            high.append(found.astype(BF16).astype(F32))
            low.append(found - high[-1])
        both = [jnp.concatenate(high, axis=1), jnp.concatenate(low, axis=1)]
        return jnp.concatenate(both, axis=0).astype(BF16)

    total = jnp.zeros(out_ref.shape, F32)
    now = columns(0)
    for i in range(steps):
        here = slice(i * tall, (i + 1) * tall)
        term = jnp.dot(now, high_ref[here, :], preferred_element_type=F32)
        small = jnp.dot(now[:rows], low_ref[here, :], preferred_element_type=F32)
        if i < steps - 1:
            now = columns(i + 1)
        total = total + (term[:rows] + (term[rows:] + small))
    out_ref[...] = total


def finish(pair_adv, pair_mode, parts, high, low, advect_count, scale_factor):
    pairs, snaps = high.shape
    _, rows, columns = parts[0][0].shape
    blocks = len(parts)
    counts = [len(part) for part in parts]
    terms = [term for part in parts for term in part]
    per_block = columns // advect_count
    return pl.pallas_call(
        functools.partial(finish_kernel, advect_count, per_block, scale_factor, counts),
        in_specs=[whole()] * (4 + len(terms)),
        out_specs=[whole(), whole()],
        out_shape=[
            jax.ShapeDtypeStruct((rows, advect_count, blocks * per_block), F32),
            jax.ShapeDtypeStruct((rows, snaps), F32),
        ],
        scratch_shapes=[pltpu.VMEM((blocks, rows, columns), F32)],
        compiler_params=params(8),
        cost_estimate=SHORT,
        name="finish",
    )(pair_adv.reshape(1, pairs), pair_mode.reshape(1, pairs), *terms, high, low)


def shards(pod_modes, slab_map, slab_volume, advect_index, pair_adv, pair_mode, pair_amp):
    comps, mode_block, planes, rows_y, width = pod_modes.shape
    mode_devs = lax.axis_size("mode")
    cell_devs = lax.axis_size("cell")
    advect_count = advect_index.shape[0]
    scale_factor = float(planes * rows_y * cell_devs * width) ** (-0.5)
    me = lax.axis_index("mode")
    rows_here = mode_block // cell_devs

    flat = pod_modes.reshape(comps, mode_block, planes * rows_y, width)
    half = mode_block // 2
    first, held = lead(flat, advect_index, (), planes, rows_y, 0, half, True)
    own = [first]
    rows, before = {}, own[0]
    for r in [rows_y - 1, *range(rows_y - 1)]:
        rows[r] = edge(held, before, planes, rows_y, r)
        before = rows[r]
    own += lead(held, advect_index, (before,), planes, rows_y, half, mode_block - half, False)
    weight = weights(slab_map, slab_volume, own[1])
    arrived = [[shifted(block, "mode", s, mode_devs, 1) for block in own] for s in range(1, mode_devs)]
    up = [(i, i + 1) for i in range(cell_devs - 1)]
    rows[-1] = lax.ppermute(rows[rows_y - 1], "cell", up)
    rows[rows_y] = lax.ppermute(rows[0], "cell", [(j, i) for i, j in up])
    leads = [own[0]] + [block[0] for block in arrived]
    right = []
    for r in range(rows_y):
        if right:
            right[-1], rows[r + 1] = lax.optimization_barrier((right[-1], rows[r + 1]))
        block = advected(leads, rows[r], rows[r - 1], rows[r + 1], weight, rows_y, r, advect_count)
        right.append(block.reshape(-1, block.shape[-1]))

    sizes = stages(cell_devs)
    early, last = min(1, len(sizes)), len(sizes) - 1

    def summed(parts, first, end, sizes):
        for number in range(first, min(end, len(sizes))):
            parts = stage(parts, number, sizes)
        return list(parts)

    pairwise = sizes[:-1] + [2, 2] if sizes[-1] == 4 else sizes
    mine = summed(contract(own, right, pairwise), 0, early, pairwise)
    mine[0], arrived = lax.optimization_barrier((mine[0], arrived))
    mine = summed(mine, early, early + 1, pairwise)
    result = []
    for s in range(1, mode_devs):
        block = contract(arrived[s - 1], right, sizes)
        if s == 1:
            mine, block = lax.optimization_barrier((mine, block))
        block = stage(summed(block, 0, last - 1, sizes), last - 1, sizes, True)
        if s == 1:
            mine = summed(mine, early + 1, early + 2, pairwise)
            mine = summed(mine, early + 2, len(pairwise), pairwise)
            block, pair_amp = lax.optimization_barrier((block, pair_amp))
            mine, pair_amp = lax.optimization_barrier((mine, pair_amp))
            result.append(mine)
        span = math.prod(sizes[:last])
        result.append([shifted(b, "cell", n, sizes[last], span, mode_devs - s) for n, b in enumerate(block)])
    high, low = prepare(pair_amp)
    tensor, response = finish(pair_adv, pair_mode, result, high, low, advect_count, scale_factor)
    return (tensor, response)


def solution(mesh):
    in_specs = (P(None, "mode", None, "cell", None), P(None, "cell", None), P(), P(), P(), P(), P())
    out_specs = (P(("mode", "cell"), None, None), P(("mode", "cell"), None))
    return jax.shard_map(shards, mesh=mesh, in_specs=in_specs, out_specs=out_specs, check_vma=False)
```

```python
import functools
import math

import jax
import jax.numpy as jnp
from jax import lax
from jax.experimental import pallas as pl
from jax.experimental.pallas import tpu as pltpu
from jax.sharding import PartitionSpec as P

LANES = 128
F32 = jnp.float32
BF16 = jnp.bfloat16


def whole(memory_space=pltpu.VMEM):
    return pl.BlockSpec(memory_space=memory_space)


def params(mib):
    return pltpu.CompilerParams(vmem_limit_bytes=mib * 2**20)


SHORT = pl.CostEstimate(flops=1, bytes_accessed=1, transcendentals=0)


def lead_places(comps, advect_count, lanes):
    pairs = -(-advect_count // 2)
    spot = [divmod(c * pairs + j, lanes // LANES) for c in range(comps) for j in range(pairs)]
    return pairs, [(row * 16, lane * LANES) for row, lane in spot]


def lead_kernel(planes, rows_y, r, advect_count, index_ref, pods_ref, out_ref, held_ref, wide):
    held_ref[...] = pods_ref[...]
    comps, modes, cells, _ = pods_ref.shape
    base = lax.axis_index("mode") * modes
    extra = out_ref.shape[0] - modes
    pairs, places = lead_places(comps, advect_count, out_ref.shape[1])
    out_ref[:extra, :] = jnp.zeros((extra, out_ref.shape[1]), BF16)
    for c in range(comps):
        wide[...] = pods_ref[c].astype(F32).reshape(modes * cells, LANES)
        for p in range(planes):
            value = wide[pl.ds(p * rows_y + r, modes, stride=cells), :]
            at = (c * planes + p) * LANES
            out_ref[extra:, at : at + LANES] = value.astype(BF16)
        for pair in range(pairs):
            blocks = []
            for j in (2 * pair, 2 * pair + 1):
                local = index_ref[min(j, advect_count - 1)] - base
                inside = jnp.logical_and(local >= 0, local < modes)
                row = pl.multiple_of(jnp.clip(local, 0, modes - 1) * cells, cells)
                blocks.append(jnp.where(inside, wide[pl.ds(row, cells), :], 0.0))
            row, lane = places[c * pairs + pair]
            out_ref[row : row + 2 * cells, lane : lane + LANES] = jnp.concatenate(blocks, axis=0).astype(BF16)


def lead(flat, advect_index, planes, rows_y, r):
    comps, modes, cells, width = flat.shape
    lanes = comps * planes * width
    _, places = lead_places(comps, advect_index.shape[0], lanes)
    return pl.pallas_call(
        functools.partial(lead_kernel, planes, rows_y, r, advect_index.shape[0]),
        in_specs=[whole(pltpu.SMEM), whole()],
        out_specs=[whole()] * 2,
        out_shape=[
            jax.ShapeDtypeStruct((places[-1][0] + 16 + modes, lanes), BF16),
            jax.ShapeDtypeStruct(flat.shape, BF16),
        ],
        scratch_shapes=[pltpu.VMEM((modes * cells, width), F32)],
        compiler_params=params(8),
        cost_estimate=SHORT,
        name="lead",
    )(advect_index, flat)


def edge_kernel(planes, rows_y, r, pods_ref, after_ref, out_ref, wide):
    comps, modes, cells, _ = pods_ref.shape
    for c in range(comps):
        wide[...] = pods_ref[c].astype(F32).reshape(modes * cells, LANES)
        for p in range(planes):
            value = wide[pl.ds(p * rows_y + r, modes, stride=cells), :]
            at = (c * planes + p) * LANES
            out_ref[:, at : at + LANES] = value.astype(BF16)


def edge(flat, after, planes, rows_y, r):
    comps, modes, cells, width = flat.shape
    return pl.pallas_call(
        functools.partial(edge_kernel, planes, rows_y, r),
        in_specs=[whole(), whole(pl.ANY)],
        out_specs=whole(),
        out_shape=jax.ShapeDtypeStruct((modes, comps * planes * width), BF16),
        scratch_shapes=[pltpu.VMEM((modes * cells, width), F32)],
        compiler_params=params(8),
        cost_estimate=SHORT,
        name="edge",
    )(flat, after)


def weight_kernel(volume_ref, map_ref, after_ref, out_ref):
    slabs = map_ref[...]
    weight = jnp.zeros(slabs.shape, F32)
    for level in range(volume_ref.shape[0]):
        weight = jnp.where(slabs == level, volume_ref[level], weight)
    out_ref[...] = weight


def weights(slab_map, slab_volume, after):
    planes, rows_y, width = slab_map.shape
    shape = (planes * rows_y, width)
    return pl.pallas_call(
        weight_kernel,
        in_specs=[whole(pltpu.SMEM), whole(), whole(pl.ANY)],
        out_specs=whole(),
        out_shape=jax.ShapeDtypeStruct(shape, F32),
        compiler_params=params(8),
        cost_estimate=SHORT,
        name="weights",
    )(slab_volume, slab_map.reshape(shape), after)


def advected_kernel(comps, planes, rows_y, r, tall, weight_ref, here_ref, under_ref, over_ref, *refs):
    lead_refs, out_ref, weighted = refs[:-2], refs[-2], refs[-1]
    advect_count = out_ref.shape[0]
    modes = here_ref.shape[0]
    cells = planes * rows_y
    weight = weight_ref[...]
    pairs, places = lead_places(comps, advect_count, lead_refs[0].shape[1])
    for d in range(comps):
        for pair in range(pairs):
            row, lane = places[d * pairs + pair]
            both = jnp.zeros((2 * cells, LANES), F32)
            for ref in lead_refs:
                both = both + ref[row : row + 2 * cells, lane : lane + LANES].astype(F32)
            for k in range(min(2, advect_count - 2 * pair)):
                weighted[d, 2 * pair + k] = 0.5 * (both[k * cells : (k + 1) * cells] * weight)

    def difference(x, y):
        return (x - y).astype(F32)

    @pl.loop(0, modes // tall)
    def _(b):
        here = pl.ds(pl.multiple_of(b * tall, tall), tall)

        def at(ref, k, p):
            lane = (k * planes + p) * LANES
            return ref[here, lane : lane + LANES]

        for k in range(comps):
            line = [at(here_ref, k, p) for p in range(planes)]
            for p in range(planes):
                grads = (
                    difference(line[(p + 1) % planes], line[(p - 1) % planes]),
                    difference(at(over_ref, k, p), at(under_ref, k, p)),
                    difference(pltpu.roll(line[p], LANES - 1, 1), pltpu.roll(line[p], 1, 1)),
                )
                cell = p * rows_y + r
                lane = (k * planes + p) * LANES
                for j in range(advect_count):
                    total = weighted[0, j, cell : cell + 1, :] * grads[0]
                    for d in range(1, comps):
                        total = total + weighted[d, j, cell : cell + 1, :] * grads[d]
                    out_ref[j, here, lane : lane + LANES] = total.astype(BF16)


def advected(leads, here, under, over, weight, rows_y, r, advect_count):
    cells, width = weight.shape
    planes = cells // rows_y
    modes, depth = here.shape
    comps = depth // (planes * width)
    return pl.pallas_call(
        functools.partial(advected_kernel, comps, planes, rows_y, r, 32),
        in_specs=[whole()] * (len(leads) + 4),
        out_specs=whole(),
        out_shape=jax.ShapeDtypeStruct((advect_count, modes, depth), BF16),
        scratch_shapes=[pltpu.VMEM((comps, advect_count, cells, width), F32)],
        compiler_params=params(8),
        cost_estimate=SHORT,
        name="advected",
    )(weight, here, under, over, *leads)


def digits(number, sizes):
    ways, span = sizes[number], math.prod(sizes[:number])
    own = lax.axis_index("cell") // span % ways
    return [lax.rem(own + s, ways) for s in range(ways)]


def begin_kernel(wide, left_ref, right_ref, out_ref):
    extra = left_ref.shape[0] - out_ref.shape[0]
    left = left_ref[extra:, :]
    for n in range(right_ref.shape[0] // wide):
        here = slice(n * wide, (n + 1) * wide)
        out_ref[:, here] = lax.dot_general(
            left, right_ref[here, :], (((1,), (1,)), ((), ())), preferred_element_type=F32
        )


def begin(left, right, rows):
    columns = right.shape[0]
    return pl.pallas_call(
        functools.partial(begin_kernel, min(columns, 256)),
        in_specs=[whole()] * 2,
        out_specs=whole(),
        out_shape=jax.ShapeDtypeStruct((rows, columns), F32),
        compiler_params=params(8),
        cost_estimate=SHORT,
        name="begin",
    )(left, right)


def contract_kernel(sizes, wide, count, begun, pieces, *refs):
    left_refs, right_refs = refs[:count], refs[count : 2 * count]
    outs, scratch = refs[2 * count + begun : -1], refs[-1]
    columns = right_refs[0].shape[0]
    places = digits(0, sizes)
    left = jnp.concatenate([ref[...] for ref in left_refs], axis=1)
    for n in range(columns // wide):
        here = slice(n * wide, (n + 1) * wide)
        right = jnp.concatenate([ref[here, :] for ref in right_refs], axis=1)
        value = lax.dot_general(left, right, (((1,), (1,)), ((), ())), preferred_element_type=F32)
        if begun:
            value = value + refs[2 * count][:, here]
        scratch[n % 2] = value.reshape(scratch.shape[1:])
        for q in range(outs[0].shape[0]):
            outs[0][q, :, here] = scratch[n % 2, q * sizes[0] + places[0]]
            for s, place in enumerate(places[1:]):
                piece, at = divmod(n * wide, columns // pieces)
                out = outs[1 + s * pieces + piece]
                out[q, :, at : at + wide] = scratch[n % 2, q * sizes[0] + place].astype(BF16)


def contract(left, right, sizes, pieces=1, begun=()):
    columns = right[0].shape[0]
    rows = left[0].shape[0]
    owners = math.prod(sizes)
    wide = min(columns, 256)
    pieces = pieces if columns // wide % pieces == 0 else 1
    shape = (owners // sizes[0], rows // owners, columns)
    part = (*shape[:2], columns // pieces)
    kept, *sent = pl.pallas_call(
        functools.partial(contract_kernel, sizes, wide, len(left), len(begun), pieces),
        in_specs=[whole()] * (2 * len(left) + len(begun)),
        out_specs=[whole()] * (1 + (sizes[0] - 1) * pieces),
        out_shape=[jax.ShapeDtypeStruct(shape, F32)]
        + [jax.ShapeDtypeStruct(part, BF16)] * ((sizes[0] - 1) * pieces),
        scratch_shapes=[pltpu.VMEM((2, owners, rows // owners, wide), F32)],
        compiler_params=params(8),
        cost_estimate=SHORT,
        name="contract",
    )(*left, *right, *begun)
    return [kept] + [sent[s * pieces : (s + 1) * pieces] for s in range(sizes[0] - 1)]


def fold_kernel(number, sizes, counts, *refs):
    kept_ref, arrived_refs, outs = refs[0], iter(refs[1 : 1 + sum(counts)]), refs[1 + sum(counts) :]
    arrived = [[next(arrived_refs) for _ in range(count)] for count in counts]
    places = [0] if number == len(sizes) else digits(number, sizes)
    ways = len(places)
    for q in range(kept_ref.shape[0] // ways):
        for out, place in zip(outs, places):
            total = kept_ref[q * ways + place]
            for pieces in arrived:
                values = [ref[q * ways + place].astype(F32) for ref in pieces]
                total = total + jnp.concatenate(values, axis=-1)
            out[q] = total.astype(out.dtype)


def fold(kept, arrived, number, sizes, all_leave=False):
    ways = 1 if number == len(sizes) else sizes[number]
    shape = (kept.shape[0] // ways, *kept.shape[1:])
    return pl.pallas_call(
        functools.partial(fold_kernel, number, sizes, [len(pieces) for pieces in arrived]),
        in_specs=[whole()] * (1 + sum(len(pieces) for pieces in arrived)),
        out_specs=[whole()] * ways,
        out_shape=[jax.ShapeDtypeStruct(shape, BF16 if s or all_leave else F32) for s in range(ways)],
        compiler_params=params(8),
        cost_estimate=SHORT,
        name="fold",
    )(kept, *[piece for pieces in arrived for piece in pieces])


def shifted(block, axis, distance, size, span, turn=0):
    reach, turns = lax.axis_size(axis), lax.axis_size("mode") if turn else 1
    route = []
    for i in range(reach):
        digit = i // span % size
        to = i + ((digit + distance) % size - digit) * span
        route += [(i * turns + m, to * turns + (m + turn) % turns) for m in range(turns)]
    return lax.ppermute(block, (axis, "mode") if turn else axis, route)


def stages(count):
    sizes = []
    while count % 4 == 0 and count > 4:
        sizes, count = sizes + [4], count // 4
    if count == 4:
        sizes, count = sizes + [2], 2
    return [count] + sizes[::-1] if count > 1 else sizes[::-1]


def stage(parts, number, sizes, all_leave=False):
    span = math.prod(sizes[:number])
    arrived = []
    for s, part in enumerate(parts[1:]):
        pieces = part if isinstance(part, list) else [part]
        arrived.append([shifted(piece, "cell", s + 1, sizes[number], span) for piece in pieces])
    return fold(parts[0], arrived, number + 1, sizes, all_leave)


def prepare_kernel(amp_ref, high_ref, low_ref, amps, sems):
    steps, tall, _ = amps.shape
    copies = []
    for i in range(steps):
        copies.append(pltpu.make_async_copy(amp_ref.at[pl.ds(i * tall, tall)], amps.at[i], sems.at[i]))
        copies[-1].start()
    for i in range(steps):
        copies[i].wait()
        amp = amps[i]
        high = amp.astype(BF16)
        high_ref[i * tall : (i + 1) * tall, :] = high
        low_ref[i * tall : (i + 1) * tall, :] = (amp - high.astype(F32)).astype(BF16)


def prepare(amp):
    pairs, snaps = amp.shape
    tall = 256 if pairs % 256 == 0 else pairs
    return pl.pallas_call(
        prepare_kernel,
        in_specs=[whole(pltpu.HBM)],
        out_specs=[whole()] * 2,
        out_shape=[jax.ShapeDtypeStruct(amp.shape, BF16)] * 2,
        scratch_shapes=[
            pltpu.VMEM((pairs // tall, tall, snaps), F32),
            pltpu.SemaphoreType.DMA((pairs // tall,)),
        ],
        compiler_params=params(24),
        cost_estimate=pl.CostEstimate(flops=4 * amp.size, bytes_accessed=8 * amp.size, transcendentals=0),
        name="prepare",
    )(amp)


def finish_kernel(advect_count, per_block, scale_factor, counts, adv_ref, mode_ref, *refs):
    *part_refs, high_ref, low_ref, tensor_ref, out_ref, flat = refs
    blocks, rows = flat.shape[0], flat.shape[1]
    me = lax.axis_index("mode")
    tall = 512 if high_ref.shape[0] % 512 == 0 else high_ref.shape[0]
    steps = high_ref.shape[0] // tall
    terms = iter(part_refs)
    for s, count in enumerate(counts):
        total = next(terms)[0].astype(F32)
        for _ in range(count - 1):
            total = total + next(terms)[0].astype(F32)
        flat[s] = total * scale_factor
    for b in range(blocks):
        for j in range(advect_count):
            at = slice(j * per_block, (j + 1) * per_block)
            value = flat[0, :, at]
            for s in range(1, blocks):
                value = jnp.where(lax.rem(me + s, blocks) == b, flat[s, :, at], value)
            tensor_ref[:, j, b * per_block : (b + 1) * per_block] = value

    groups = flat.shape[2] // LANES

    def columns(i):
        high, low = [], []
        for g in range(i * tall // LANES, (i + 1) * tall // LANES):
            here = slice(g * LANES, (g + 1) * LANES)
            mode = mode_ref[:, here]
            part = lax.rem(mode // per_block - me + blocks, blocks)
            slot = (part * advect_count + adv_ref[:, here]) * per_block + lax.rem(mode, per_block)
            lane = jnp.broadcast_to(lax.rem(slot, LANES), (rows, LANES))
            group = jnp.broadcast_to(slot // LANES, (rows, LANES))
            found = jnp.zeros((rows, LANES), F32)
            for b in range(blocks):
                for s in range(groups):
                    source = flat[b, :, s * LANES : (s + 1) * LANES]
                    taken = jnp.take_along_axis(source, lane, axis=1)
                    found = jnp.where(group == b * groups + s, taken, found)
            high.append(found.astype(BF16).astype(F32))
            low.append(found - high[-1])
        both = [jnp.concatenate(high, axis=1), jnp.concatenate(low, axis=1)]
        return jnp.concatenate(both, axis=0).astype(BF16)

    total = jnp.zeros(out_ref.shape, F32)
    now = columns(0)
    for i in range(steps):
        here = slice(i * tall, (i + 1) * tall)
        term = jnp.dot(now, high_ref[here, :], preferred_element_type=F32)
        small = jnp.dot(now[:rows], low_ref[here, :], preferred_element_type=F32)
        if i < steps - 1:
            now = columns(i + 1)
        total = total + (term[:rows] + (term[rows:] + small))
    out_ref[...] = total


def finish(pair_adv, pair_mode, parts, high, low, advect_count, scale_factor):
    pairs, snaps = high.shape
    _, rows, columns = parts[0][0].shape
    blocks = len(parts)
    counts = [len(part) for part in parts]
    terms = [term for part in parts for term in part]
    per_block = columns // advect_count
    return pl.pallas_call(
        functools.partial(finish_kernel, advect_count, per_block, scale_factor, counts),
        in_specs=[whole()] * (4 + len(terms)),
        out_specs=[whole(), whole()],
        out_shape=[
            jax.ShapeDtypeStruct((rows, advect_count, blocks * per_block), F32),
            jax.ShapeDtypeStruct((rows, snaps), F32),
        ],
        scratch_shapes=[pltpu.VMEM((blocks, rows, columns), F32)],
        compiler_params=params(8),
        cost_estimate=SHORT,
        name="finish",
    )(pair_adv.reshape(1, pairs), pair_mode.reshape(1, pairs), *terms, high, low)


def shards(pod_modes, slab_map, slab_volume, advect_index, pair_adv, pair_mode, pair_amp):
    comps, mode_block, planes, rows_y, width = pod_modes.shape
    mode_devs = lax.axis_size("mode")
    cell_devs = lax.axis_size("cell")
    advect_count = advect_index.shape[0]
    scale_factor = float(planes * rows_y * cell_devs * width) ** (-0.5)
    me = lax.axis_index("mode")
    rows_here = mode_block // cell_devs

    flat = pod_modes.reshape(comps, mode_block, planes * rows_y, width)
    first, held = lead(flat, advect_index, planes, rows_y, rows_y - 1)
    rows, before = {}, first
    for r in [rows_y - 1, *range(rows_y - 1)]:
        rows[r] = edge(held, before, planes, rows_y, r)
        before = rows[r]
    weight = weights(slab_map, slab_volume, before)
    own = [rows[r] for r in range(rows_y)]
    ahead = [shifted(first, "mode", s, mode_devs, 1) for s in range(1, mode_devs)]
    arrived = [[shifted(block, "mode", s, mode_devs, 1) for block in own[:-1]] for s in range(1, mode_devs)]
    up = [(i, i + 1) for i in range(cell_devs - 1)]
    rows[-1] = lax.ppermute(rows[rows_y - 1], "cell", up)
    rows[rows_y] = lax.ppermute(rows[0], "cell", [(j, i) for i, j in up])
    leads = [first] + ahead
    right = []
    for r in range(rows_y):
        if right:
            right[-1], rows[r + 1] = lax.optimization_barrier((right[-1], rows[r + 1]))
        block = advected(leads, rows[r], rows[r - 1], rows[r + 1], weight, rows_y, r, advect_count)
        right.append(block.reshape(-1, block.shape[-1]))

    sizes = stages(cell_devs)
    early, last = min(1, len(sizes)), len(sizes) - 1

    def summed(parts, first, end, sizes):
        for number in range(first, min(end, len(sizes))):
            parts = stage(parts, number, sizes)
        return list(parts)

    pairwise = sizes[:-1] + [2, 2] if sizes[-1] == 4 else sizes
    mine = contract(own, right, pairwise)
    mine[0], ahead = lax.optimization_barrier((mine[0], ahead))
    begun = begin(ahead[0], right[-1], mode_block)
    mine = summed(mine, 0, early, pairwise)
    mine, begun = lax.optimization_barrier((mine, begun))
    mine[0], arrived = lax.optimization_barrier((mine[0], arrived))
    mine = summed(mine, early, early + 1, pairwise)
    result = []
    for s in range(1, mode_devs):
        begun = begun if s == 1 else begin(ahead[s - 1], right[-1], mode_block)
        block = contract(arrived[s - 1], right[:-1], sizes, 4, [begun])
        block = summed(block, 0, early, sizes)
        if s == 1:
            mine, block = lax.optimization_barrier((mine, block))
        block = stage(summed(block, early, last - 1, sizes), last - 1, sizes, True)
        if s == 1:
            mine = summed(mine, early + 1, early + 2, pairwise)
            mine = summed(mine, early + 2, len(pairwise), pairwise)
            block, pair_amp = lax.optimization_barrier((block, pair_amp))
            mine, pair_amp = lax.optimization_barrier((mine, pair_amp))
            result.append(mine)
        span = math.prod(sizes[:last])
        result.append([shifted(b, "cell", n, sizes[last], span, mode_devs - s) for n, b in enumerate(block)])
    high, low = prepare(pair_amp)
    tensor, response = finish(pair_adv, pair_mode, result, high, low, advect_count, scale_factor)
    return (tensor, response)


def solution(mesh):
    in_specs = (P(None, "mode", None, "cell", None), P(None, "cell", None), P(), P(), P(), P(), P())
    out_specs = (P(("mode", "cell"), None, None), P(("mode", "cell"), None))
    return jax.shard_map(shards, mesh=mesh, in_specs=in_specs, out_specs=out_specs, check_vma=False)
```

```python
import functools
import math

import jax
import jax.numpy as jnp
from jax import lax
from jax.experimental import pallas as pl
from jax.experimental.pallas import tpu as pltpu
from jax.sharding import PartitionSpec as P

LANES = 128
F32 = jnp.float32
BF16 = jnp.bfloat16


def whole(memory_space=pltpu.VMEM):
    return pl.BlockSpec(memory_space=memory_space)


def params(mib):
    return pltpu.CompilerParams(vmem_limit_bytes=mib * 2**20)


SHORT = pl.CostEstimate(flops=1, bytes_accessed=1, transcendentals=0)


def lead_places(comps, advect_count, lanes):
    pairs = -(-advect_count // 2)
    spot = [divmod(c * pairs + j, lanes // LANES) for c in range(comps) for j in range(pairs)]
    return pairs, [(row * 16, lane * LANES) for row, lane in spot]


def lead_kernel(planes, rows_y, r, advect_count, index_ref, pods_ref, out_ref, held_ref, wide):
    held_ref[...] = pods_ref[...]
    comps, modes, cells, _ = pods_ref.shape
    base = lax.axis_index("mode") * modes
    extra = out_ref.shape[0] - modes
    pairs, places = lead_places(comps, advect_count, out_ref.shape[1])
    out_ref[:extra, :] = jnp.zeros((extra, out_ref.shape[1]), BF16)
    for c in range(comps):
        wide[...] = pods_ref[c].astype(F32).reshape(modes * cells, LANES)
        for p in range(planes):
            value = wide[pl.ds(p * rows_y + r, modes, stride=cells), :]
            at = (c * planes + p) * LANES
            out_ref[extra:, at : at + LANES] = value.astype(BF16)
        for pair in range(pairs):
            blocks = []
            for j in (2 * pair, 2 * pair + 1):
                local = index_ref[min(j, advect_count - 1)] - base
                inside = jnp.logical_and(local >= 0, local < modes)
                row = pl.multiple_of(jnp.clip(local, 0, modes - 1) * cells, cells)
                blocks.append(jnp.where(inside, wide[pl.ds(row, cells), :], 0.0))
            row, lane = places[c * pairs + pair]
            out_ref[row : row + 2 * cells, lane : lane + LANES] = jnp.concatenate(blocks, axis=0).astype(BF16)


def lead(flat, advect_index, planes, rows_y, r):
    comps, modes, cells, width = flat.shape
    lanes = comps * planes * width
    _, places = lead_places(comps, advect_index.shape[0], lanes)
    return pl.pallas_call(
        functools.partial(lead_kernel, planes, rows_y, r, advect_index.shape[0]),
        in_specs=[whole(pltpu.SMEM), whole()],
        out_specs=[whole()] * 2,
        out_shape=[
            jax.ShapeDtypeStruct((places[-1][0] + 16 + modes, lanes), BF16),
            jax.ShapeDtypeStruct(flat.shape, BF16),
        ],
        scratch_shapes=[pltpu.VMEM((modes * cells, width), F32)],
        compiler_params=params(8),
        cost_estimate=SHORT,
        name="lead",
    )(advect_index, flat)


def edge_kernel(planes, rows_y, r, pods_ref, after_ref, out_ref, wide):
    comps, modes, cells, _ = pods_ref.shape
    for c in range(comps):
        wide[...] = pods_ref[c].astype(F32).reshape(modes * cells, LANES)
        for p in range(planes):
            value = wide[pl.ds(p * rows_y + r, modes, stride=cells), :]
            at = (c * planes + p) * LANES
            out_ref[:, at : at + LANES] = value.astype(BF16)


def edge(flat, after, planes, rows_y, r):
    comps, modes, cells, width = flat.shape
    return pl.pallas_call(
        functools.partial(edge_kernel, planes, rows_y, r),
        in_specs=[whole(), whole(pl.ANY)],
        out_specs=whole(),
        out_shape=jax.ShapeDtypeStruct((modes, comps * planes * width), BF16),
        scratch_shapes=[pltpu.VMEM((modes * cells, width), F32)],
        compiler_params=params(8),
        cost_estimate=SHORT,
        name="edge",
    )(flat, after)


def weight_kernel(volume_ref, map_ref, after_ref, out_ref):
    slabs = map_ref[...]
    weight = jnp.zeros(slabs.shape, F32)
    for level in range(volume_ref.shape[0]):
        weight = jnp.where(slabs == level, volume_ref[level], weight)
    out_ref[...] = weight


def weights(slab_map, slab_volume, after):
    planes, rows_y, width = slab_map.shape
    shape = (planes * rows_y, width)
    return pl.pallas_call(
        weight_kernel,
        in_specs=[whole(pltpu.SMEM), whole(), whole(pl.ANY)],
        out_specs=whole(),
        out_shape=jax.ShapeDtypeStruct(shape, F32),
        compiler_params=params(8),
        cost_estimate=SHORT,
        name="weights",
    )(slab_volume, slab_map.reshape(shape), after)


def advected_kernel(comps, planes, rows_y, r, tall, weight_ref, here_ref, under_ref, over_ref, *refs):
    lead_refs, out_ref, weighted = refs[:-2], refs[-2], refs[-1]
    advect_count = out_ref.shape[0]
    modes = here_ref.shape[0]
    cells = planes * rows_y
    weight = weight_ref[...]
    pairs, places = lead_places(comps, advect_count, lead_refs[0].shape[1])
    for d in range(comps):
        for pair in range(pairs):
            row, lane = places[d * pairs + pair]
            both = jnp.zeros((2 * cells, LANES), F32)
            for ref in lead_refs:
                both = both + ref[row : row + 2 * cells, lane : lane + LANES].astype(F32)
            for k in range(min(2, advect_count - 2 * pair)):
                weighted[d, 2 * pair + k] = 0.5 * (both[k * cells : (k + 1) * cells] * weight)

    def difference(x, y):
        return (x - y).astype(F32)

    @pl.loop(0, modes // tall, unroll=2)
    def _(b):
        here = pl.ds(pl.multiple_of(b * tall, tall), tall)

        def at(ref, k, p):
            lane = (k * planes + p) * LANES
            return ref[here, lane : lane + LANES]

        for k in range(comps):
            line = [at(here_ref, k, p) for p in range(planes)]
            for p in range(planes):
                grads = (
                    difference(line[(p + 1) % planes], line[(p - 1) % planes]),
                    difference(at(over_ref, k, p), at(under_ref, k, p)),
                    difference(pltpu.roll(line[p], LANES - 1, 1), pltpu.roll(line[p], 1, 1)),
                )
                cell = p * rows_y + r
                lane = (k * planes + p) * LANES
                for j in range(advect_count):
                    total = weighted[0, j, cell : cell + 1, :] * grads[0]
                    for d in range(1, comps):
                        total = total + weighted[d, j, cell : cell + 1, :] * grads[d]
                    out_ref[j, here, lane : lane + LANES] = total.astype(BF16)


def advected(leads, here, under, over, weight, rows_y, r, advect_count):
    cells, width = weight.shape
    planes = cells // rows_y
    modes, depth = here.shape
    comps = depth // (planes * width)
    return pl.pallas_call(
        functools.partial(advected_kernel, comps, planes, rows_y, r, 32),
        in_specs=[whole()] * (len(leads) + 4),
        out_specs=whole(),
        out_shape=jax.ShapeDtypeStruct((advect_count, modes, depth), BF16),
        scratch_shapes=[pltpu.VMEM((comps, advect_count, cells, width), F32)],
        compiler_params=params(8),
        cost_estimate=SHORT,
        name="advected",
    )(weight, here, under, over, *leads)


def digits(number, sizes):
    ways, span = sizes[number], math.prod(sizes[:number])
    own = lax.axis_index("cell") // span % ways
    return [lax.rem(own + s, ways) for s in range(ways)]


def begin_kernel(wide, left_ref, right_ref, out_ref):
    extra = left_ref.shape[0] - out_ref.shape[0]
    left = left_ref[extra:, :]
    for n in range(right_ref.shape[0] // wide):
        here = slice(n * wide, (n + 1) * wide)
        out_ref[:, here] = lax.dot_general(
            left, right_ref[here, :], (((1,), (1,)), ((), ())), preferred_element_type=F32
        )


def begin(left, right, rows):
    columns = right.shape[0]
    return pl.pallas_call(
        functools.partial(begin_kernel, min(columns, 256)),
        in_specs=[whole()] * 2,
        out_specs=whole(),
        out_shape=jax.ShapeDtypeStruct((rows, columns), F32),
        compiler_params=params(8),
        cost_estimate=SHORT,
        name="begin",
    )(left, right)


def contract_kernel(sizes, wide, count, begun, pieces, *refs):
    left_refs, right_refs = refs[:count], refs[count : 2 * count]
    outs, scratch = refs[2 * count + begun : -1], refs[-1]
    columns = right_refs[0].shape[0]
    places = digits(0, sizes)
    left = jnp.concatenate([ref[...] for ref in left_refs], axis=1)
    for n in range(columns // wide):
        here = slice(n * wide, (n + 1) * wide)
        right = jnp.concatenate([ref[here, :] for ref in right_refs], axis=1)
        value = lax.dot_general(left, right, (((1,), (1,)), ((), ())), preferred_element_type=F32)
        if begun:
            value = value + refs[2 * count][:, here]
        scratch[n % 2] = value.reshape(scratch.shape[1:])
        for q in range(outs[0].shape[0]):
            outs[0][q, :, here] = scratch[n % 2, q * sizes[0] + places[0]]
            for s, place in enumerate(places[1:]):
                piece, at = divmod(n * wide, columns // pieces)
                out = outs[1 + s * pieces + piece]
                out[q, :, at : at + wide] = scratch[n % 2, q * sizes[0] + place].astype(BF16)


def contract(left, right, sizes, pieces=1, begun=()):
    columns = right[0].shape[0]
    rows = left[0].shape[0]
    owners = math.prod(sizes)
    wide = min(columns, 256)
    pieces = pieces if columns // wide % pieces == 0 else 1
    shape = (owners // sizes[0], rows // owners, columns)
    part = (*shape[:2], columns // pieces)
    kept, *sent = pl.pallas_call(
        functools.partial(contract_kernel, sizes, wide, len(left), len(begun), pieces),
        in_specs=[whole()] * (2 * len(left) + len(begun)),
        out_specs=[whole()] * (1 + (sizes[0] - 1) * pieces),
        out_shape=[jax.ShapeDtypeStruct(shape, F32)]
        + [jax.ShapeDtypeStruct(part, BF16)] * ((sizes[0] - 1) * pieces),
        scratch_shapes=[pltpu.VMEM((2, owners, rows // owners, wide), F32)],
        compiler_params=params(8),
        cost_estimate=SHORT,
        name="contract",
    )(*left, *right, *begun)
    return [kept] + [sent[s * pieces : (s + 1) * pieces] for s in range(sizes[0] - 1)]


def fold_kernel(number, sizes, counts, *refs):
    kept_ref, arrived_refs, outs = refs[0], iter(refs[1 : 1 + sum(counts)]), refs[1 + sum(counts) :]
    arrived = [[next(arrived_refs) for _ in range(count)] for count in counts]
    places = [0] if number == len(sizes) else digits(number, sizes)
    ways = len(places)
    for q in range(kept_ref.shape[0] // ways):
        for out, place in zip(outs, places):
            total = kept_ref[q * ways + place]
            for pieces in arrived:
                values = [ref[q * ways + place].astype(F32) for ref in pieces]
                total = total + jnp.concatenate(values, axis=-1)
            out[q] = total.astype(out.dtype)


def fold(kept, arrived, number, sizes, all_leave=False):
    ways = 1 if number == len(sizes) else sizes[number]
    shape = (kept.shape[0] // ways, *kept.shape[1:])
    return pl.pallas_call(
        functools.partial(fold_kernel, number, sizes, [len(pieces) for pieces in arrived]),
        in_specs=[whole()] * (1 + sum(len(pieces) for pieces in arrived)),
        out_specs=[whole()] * ways,
        out_shape=[jax.ShapeDtypeStruct(shape, BF16 if s or all_leave else F32) for s in range(ways)],
        compiler_params=params(8),
        cost_estimate=SHORT,
        name="fold",
    )(kept, *[piece for pieces in arrived for piece in pieces])


def shifted(block, axis, distance, size, span, turn=0):
    reach, turns = lax.axis_size(axis), lax.axis_size("mode") if turn else 1
    route = []
    for i in range(reach):
        digit = i // span % size
        to = i + ((digit + distance) % size - digit) * span
        route += [(i * turns + m, to * turns + (m + turn) % turns) for m in range(turns)]
    return lax.ppermute(block, (axis, "mode") if turn else axis, route)


def stages(count):
    sizes = []
    while count % 4 == 0 and count > 4:
        sizes, count = sizes + [4], count // 4
    if count == 4:
        sizes, count = sizes + [2], 2
    return [count] + sizes[::-1] if count > 1 else sizes[::-1]


def stage(parts, number, sizes, all_leave=False):
    span = math.prod(sizes[:number])
    arrived = []
    for s, part in enumerate(parts[1:]):
        pieces = part if isinstance(part, list) else [part]
        arrived.append([shifted(piece, "cell", s + 1, sizes[number], span) for piece in pieces])
    return fold(parts[0], arrived, number + 1, sizes, all_leave)


def columns_of(flat, first, blocks, total, found, adv, mode, me, advect_count, per_block):
    rows, groups = found.shape[0], flat.shape[2] // LANES
    part = lax.rem(mode // per_block - me + total, total)
    slot = (part * advect_count + adv) * per_block + lax.rem(mode, per_block)
    lane = jnp.broadcast_to(lax.rem(slot, LANES), (rows, LANES))
    group = jnp.broadcast_to(slot // LANES, (rows, LANES))
    for b in range(blocks):
        for s in range(groups):
            source = flat[b, :, s * LANES : (s + 1) * LANES]
            taken = jnp.take_along_axis(source, lane, axis=1)
            found = jnp.where(group == (first + b) * groups + s, taken, found)
    return found


def prepare_kernel(blocks, advect_count, per_block, scale_factor, adv_ref, mode_ref, own_ref, amp_ref, high_ref, low_ref, found_ref, flat, amps, sems):
    steps, tall, _ = amps.shape
    copies = []
    for i in range(steps):
        copies.append(pltpu.make_async_copy(amp_ref.at[pl.ds(i * tall, tall)], amps.at[i], sems.at[i]))
        copies[-1].start()
    flat[0] = own_ref[0] * scale_factor
    for g in range(found_ref.shape[1] // LANES):
        here = slice(g * LANES, (g + 1) * LANES)
        found = jnp.zeros((found_ref.shape[0], LANES), F32)
        me = lax.axis_index("mode")
        pairs = adv_ref[:, here], mode_ref[:, here]
        found_ref[:, here] = columns_of(flat, 0, 1, blocks, found, *pairs, me, advect_count, per_block)
    for i in range(steps):
        copies[i].wait()
        amp = amps[i]
        high = amp.astype(BF16)
        high_ref[i * tall : (i + 1) * tall, :] = high
        low_ref[i * tall : (i + 1) * tall, :] = (amp - high.astype(F32)).astype(BF16)


def prepare(pair_adv, pair_mode, own, amp, blocks, advect_count, scale_factor):
    pairs, snaps = amp.shape
    _, rows, columns = own.shape
    tall = 256 if pairs % 256 == 0 else pairs
    per_block = columns // advect_count
    return pl.pallas_call(
        functools.partial(prepare_kernel, blocks, advect_count, per_block, scale_factor),
        in_specs=[whole()] * 3 + [whole(pltpu.HBM)],
        out_specs=[whole()] * 3,
        out_shape=[jax.ShapeDtypeStruct(amp.shape, BF16)] * 2 + [jax.ShapeDtypeStruct((rows, pairs), F32)],
        scratch_shapes=[
            pltpu.VMEM((1, rows, columns), F32),
            pltpu.VMEM((pairs // tall, tall, snaps), F32),
            pltpu.SemaphoreType.DMA((pairs // tall,)),
        ],
        compiler_params=params(24),
        cost_estimate=pl.CostEstimate(flops=4 * amp.size, bytes_accessed=8 * amp.size, transcendentals=0),
        name="prepare",
    )(pair_adv.reshape(1, pairs), pair_mode.reshape(1, pairs), own, amp)


def finish_kernel(advect_count, per_block, scale_factor, counts, adv_ref, mode_ref, *refs):
    *part_refs, high_ref, low_ref, found_ref, tensor_ref, out_ref, flat = refs
    blocks, rows = flat.shape[0], flat.shape[1]
    me = lax.axis_index("mode")
    tall = 512 if high_ref.shape[0] % 512 == 0 else high_ref.shape[0]
    steps = high_ref.shape[0] // tall
    terms = iter(part_refs)
    for s, count in enumerate(counts):
        total = next(terms)[0].astype(F32)
        for _ in range(count - 1):
            total = total + next(terms)[0].astype(F32)
        flat[s] = total * scale_factor
    for b in range(blocks):
        for j in range(advect_count):
            at = slice(j * per_block, (j + 1) * per_block)
            value = flat[0, :, at]
            for s in range(1, blocks):
                value = jnp.where(lax.rem(me + s, blocks) == b, flat[s, :, at], value)
            tensor_ref[:, j, b * per_block : (b + 1) * per_block] = value

    def columns(i):
        high, low = [], []
        for g in range(i * tall // LANES, (i + 1) * tall // LANES):
            here = slice(g * LANES, (g + 1) * LANES)
            pairs = adv_ref[:, here], mode_ref[:, here]
            found = columns_of(
                flat.at[1:], 1, blocks - 1, blocks, found_ref[:, here], *pairs, me, advect_count, per_block
            )
            high.append(found.astype(BF16).astype(F32))
            low.append(found - high[-1])
        both = [jnp.concatenate(high, axis=1), jnp.concatenate(low, axis=1)]
        return jnp.concatenate(both, axis=0).astype(BF16)

    total = jnp.zeros(out_ref.shape, F32)
    now = columns(0)
    for i in range(steps):
        here = slice(i * tall, (i + 1) * tall)
        term = jnp.dot(now, high_ref[here, :], preferred_element_type=F32)
        small = jnp.dot(now[:rows], low_ref[here, :], preferred_element_type=F32)
        if i < steps - 1:
            now = columns(i + 1)
        total = total + (term[:rows] + (term[rows:] + small))
    out_ref[...] = total


def finish(pair_adv, pair_mode, parts, high, low, found, advect_count, scale_factor):
    pairs, snaps = high.shape
    _, rows, columns = parts[0][0].shape
    blocks = len(parts)
    counts = [len(part) for part in parts]
    terms = [term for part in parts for term in part]
    per_block = columns // advect_count
    return pl.pallas_call(
        functools.partial(finish_kernel, advect_count, per_block, scale_factor, counts),
        in_specs=[whole()] * (5 + len(terms)),
        out_specs=[whole(), whole()],
        out_shape=[
            jax.ShapeDtypeStruct((rows, advect_count, blocks * per_block), F32),
            jax.ShapeDtypeStruct((rows, snaps), F32),
        ],
        scratch_shapes=[pltpu.VMEM((blocks, rows, columns), F32)],
        compiler_params=params(8),
        cost_estimate=SHORT,
        name="finish",
    )(pair_adv.reshape(1, pairs), pair_mode.reshape(1, pairs), *terms, high, low, found)


def shards(pod_modes, slab_map, slab_volume, advect_index, pair_adv, pair_mode, pair_amp):
    comps, mode_block, planes, rows_y, width = pod_modes.shape
    mode_devs = lax.axis_size("mode")
    cell_devs = lax.axis_size("cell")
    advect_count = advect_index.shape[0]
    scale_factor = float(planes * rows_y * cell_devs * width) ** (-0.5)
    me = lax.axis_index("mode")
    rows_here = mode_block // cell_devs

    flat = pod_modes.reshape(comps, mode_block, planes * rows_y, width)
    first, held = lead(flat, advect_index, planes, rows_y, rows_y - 1)
    rows, before = {}, first
    for r in [rows_y - 1, *range(rows_y - 1)]:
        rows[r] = edge(held, before, planes, rows_y, r)
        before = rows[r]
    weight = weights(slab_map, slab_volume, before)
    own = [rows[r] for r in range(rows_y)]
    ahead = [shifted(first, "mode", s, mode_devs, 1) for s in range(1, mode_devs)]
    arrived = [[shifted(block, "mode", s, mode_devs, 1) for block in own[:-1]] for s in range(1, mode_devs)]
    up = [(i, i + 1) for i in range(cell_devs - 1)]
    rows[-1] = lax.ppermute(rows[rows_y - 1], "cell", up)
    rows[rows_y] = lax.ppermute(rows[0], "cell", [(j, i) for i, j in up])
    leads = [first] + ahead
    right = []
    for r in range(rows_y):
        if right:
            right[-1], rows[r + 1] = lax.optimization_barrier((right[-1], rows[r + 1]))
        block = advected(leads, rows[r], rows[r - 1], rows[r + 1], weight, rows_y, r, advect_count)
        right.append(block.reshape(-1, block.shape[-1]))

    sizes = stages(cell_devs)
    early, last = min(1, len(sizes)), len(sizes) - 1

    def summed(parts, first, end, sizes):
        for number in range(first, min(end, len(sizes))):
            parts = stage(parts, number, sizes)
        return list(parts)

    pairwise = sizes[:-1] + [2, 2] if sizes[-1] == 4 else sizes
    mine = contract(own, right, pairwise)
    mine[0], ahead = lax.optimization_barrier((mine[0], ahead))
    begun = begin(ahead[0], right[-1], mode_block)
    mine = summed(mine, 0, early, pairwise)
    mine, begun = lax.optimization_barrier((mine, begun))
    mine[0], arrived = lax.optimization_barrier((mine[0], arrived))
    mine = summed(mine, early, early + 1, pairwise)
    result = []
    for s in range(1, mode_devs):
        begun = begun if s == 1 else begin(ahead[s - 1], right[-1], mode_block)
        block = contract(arrived[s - 1], right[:-1], sizes, 4, [begun])
        block = summed(block, 0, early, sizes)
        if s == 1:
            mine, block = lax.optimization_barrier((mine, block))
        block = stage(summed(block, early, last - 1, sizes), last - 1, sizes, True)
        if s == 1:
            mine = summed(mine, early + 1, early + 2, pairwise)
            mine = summed(mine, early + 2, len(pairwise), pairwise)
            block, pair_amp = lax.optimization_barrier((block, pair_amp))
            mine, pair_amp = lax.optimization_barrier((mine, pair_amp))
            result.append(mine)
        span = math.prod(sizes[:last])
        result.append([shifted(b, "cell", n, sizes[last], span, mode_devs - s) for n, b in enumerate(block)])
    high, low, found = prepare(
        pair_adv, pair_mode, result[0][0], pair_amp, mode_devs, advect_count, scale_factor
    )
    tensor, response = finish(pair_adv, pair_mode, result, high, low, found, advect_count, scale_factor)
    return (tensor, response)


def solution(mesh):
    in_specs = (P(None, "mode", None, "cell", None), P(None, "cell", None), P(), P(), P(), P(), P())
    out_specs = (P(("mode", "cell"), None, None), P(("mode", "cell"), None))
    return jax.shard_map(shards, mesh=mesh, in_specs=in_specs, out_specs=out_specs, check_vma=False)
```

```python
import functools
import math

import jax
import jax.numpy as jnp
from jax import lax
from jax.experimental import pallas as pl
from jax.experimental.pallas import tpu as pltpu
from jax.sharding import PartitionSpec as P

LANES = 128
F32 = jnp.float32
BF16 = jnp.bfloat16


def whole(memory_space=pltpu.VMEM):
    return pl.BlockSpec(memory_space=memory_space)


def params(mib):
    return pltpu.CompilerParams(vmem_limit_bytes=mib * 2**20)


SHORT = pl.CostEstimate(flops=1, bytes_accessed=1, transcendentals=0)


def lead_places(comps, advect_count, lanes):
    pairs = -(-advect_count // 2)
    spot = [divmod(c * pairs + j, lanes // LANES) for c in range(comps) for j in range(pairs)]
    return pairs, [(row * 16, lane * LANES) for row, lane in spot]


def lead_kernel(planes, rows_y, r, advect_count, index_ref, pods_ref, out_ref, held_ref, wide):
    held_ref[...] = pods_ref[...]
    comps, modes, cells, _ = pods_ref.shape
    base = lax.axis_index("mode") * modes
    extra = out_ref.shape[0] - modes
    pairs, places = lead_places(comps, advect_count, out_ref.shape[1])
    out_ref[:extra, :] = jnp.zeros((extra, out_ref.shape[1]), BF16)
    for c in range(comps):
        wide[...] = pods_ref[c].astype(F32).reshape(modes * cells, LANES)
        for p in range(planes):
            value = wide[pl.ds(p * rows_y + r, modes, stride=cells), :]
            at = (c * planes + p) * LANES
            out_ref[extra:, at : at + LANES] = value.astype(BF16)
        for pair in range(pairs):
            blocks = []
            for j in (2 * pair, 2 * pair + 1):
                local = index_ref[min(j, advect_count - 1)] - base
                inside = jnp.logical_and(local >= 0, local < modes)
                row = pl.multiple_of(jnp.clip(local, 0, modes - 1) * cells, cells)
                blocks.append(jnp.where(inside, wide[pl.ds(row, cells), :], 0.0))
            row, lane = places[c * pairs + pair]
            out_ref[row : row + 2 * cells, lane : lane + LANES] = jnp.concatenate(blocks, axis=0).astype(BF16)


def lead(flat, advect_index, planes, rows_y, r):
    comps, modes, cells, width = flat.shape
    lanes = comps * planes * width
    _, places = lead_places(comps, advect_index.shape[0], lanes)
    return pl.pallas_call(
        functools.partial(lead_kernel, planes, rows_y, r, advect_index.shape[0]),
        in_specs=[whole(pltpu.SMEM), whole()],
        out_specs=[whole()] * 2,
        out_shape=[
            jax.ShapeDtypeStruct((places[-1][0] + 16 + modes, lanes), BF16),
            jax.ShapeDtypeStruct(flat.shape, BF16),
        ],
        scratch_shapes=[pltpu.VMEM((modes * cells, width), F32)],
        compiler_params=params(8),
        cost_estimate=SHORT,
        name="lead",
    )(advect_index, flat)


def edge_kernel(planes, rows_y, r, pods_ref, after_ref, out_ref, wide):
    comps, modes, cells, _ = pods_ref.shape
    for c in range(comps):
        wide[...] = pods_ref[c].astype(F32).reshape(modes * cells, LANES)
        for p in range(planes):
            value = wide[pl.ds(p * rows_y + r, modes, stride=cells), :]
            at = (c * planes + p) * LANES
            out_ref[:, at : at + LANES] = value.astype(BF16)


def edge(flat, after, planes, rows_y, r):
    comps, modes, cells, width = flat.shape
    return pl.pallas_call(
        functools.partial(edge_kernel, planes, rows_y, r),
        in_specs=[whole(), whole(pl.ANY)],
        out_specs=whole(),
        out_shape=jax.ShapeDtypeStruct((modes, comps * planes * width), BF16),
        scratch_shapes=[pltpu.VMEM((modes * cells, width), F32)],
        compiler_params=params(8),
        cost_estimate=SHORT,
        name="edge",
    )(flat, after)


def weight_kernel(volume_ref, map_ref, after_ref, out_ref):
    slabs = map_ref[...]
    weight = jnp.zeros(slabs.shape, F32)
    for level in range(volume_ref.shape[0]):
        weight = jnp.where(slabs == level, volume_ref[level], weight)
    out_ref[...] = weight


def weights(slab_map, slab_volume, after):
    planes, rows_y, width = slab_map.shape
    shape = (planes * rows_y, width)
    return pl.pallas_call(
        weight_kernel,
        in_specs=[whole(pltpu.SMEM), whole(), whole(pl.ANY)],
        out_specs=whole(),
        out_shape=jax.ShapeDtypeStruct(shape, F32),
        compiler_params=params(8),
        cost_estimate=SHORT,
        name="weights",
    )(slab_volume, slab_map.reshape(shape), after)


def advected_kernel(comps, planes, rows_y, r, tall, weight_ref, here_ref, under_ref, over_ref, *refs):
    lead_refs, out_ref, weighted = refs[:-2], refs[-2], refs[-1]
    advect_count = out_ref.shape[0]
    modes = here_ref.shape[0]
    cells = planes * rows_y
    weight = weight_ref[...]
    pairs, places = lead_places(comps, advect_count, lead_refs[0].shape[1])
    for d in range(comps):
        for pair in range(pairs):
            row, lane = places[d * pairs + pair]
            both = jnp.zeros((2 * cells, LANES), F32)
            for ref in lead_refs:
                both = both + ref[row : row + 2 * cells, lane : lane + LANES].astype(F32)
            for k in range(min(2, advect_count - 2 * pair)):
                weighted[d, 2 * pair + k] = 0.5 * (both[k * cells : (k + 1) * cells] * weight)

    def difference(x, y):
        return (x - y).astype(F32)

    @pl.loop(0, modes // tall, unroll=2)
    def _(b):
        here = pl.ds(pl.multiple_of(b * tall, tall), tall)

        def at(ref, k, p):
            lane = (k * planes + p) * LANES
            return ref[here, lane : lane + LANES]

        for k in range(comps):
            line = [at(here_ref, k, p) for p in range(planes)]
            for p in range(planes):
                grads = (
                    difference(line[(p + 1) % planes], line[(p - 1) % planes]),
                    difference(at(over_ref, k, p), at(under_ref, k, p)),
                    difference(pltpu.roll(line[p], LANES - 1, 1), pltpu.roll(line[p], 1, 1)),
                )
                cell = p * rows_y + r
                lane = (k * planes + p) * LANES
                for j in range(advect_count):
                    total = weighted[0, j, cell : cell + 1, :] * grads[0]
                    for d in range(1, comps):
                        total = total + weighted[d, j, cell : cell + 1, :] * grads[d]
                    out_ref[j, here, lane : lane + LANES] = total.astype(BF16)


def advected(leads, here, under, over, weight, rows_y, r, advect_count):
    cells, width = weight.shape
    planes = cells // rows_y
    modes, depth = here.shape
    comps = depth // (planes * width)
    return pl.pallas_call(
        functools.partial(advected_kernel, comps, planes, rows_y, r, 32),
        in_specs=[whole()] * (len(leads) + 4),
        out_specs=whole(),
        out_shape=jax.ShapeDtypeStruct((advect_count, modes, depth), BF16),
        scratch_shapes=[pltpu.VMEM((comps, advect_count, cells, width), F32)],
        compiler_params=params(8),
        cost_estimate=SHORT,
        name="advected",
    )(weight, here, under, over, *leads)


def digits(number, sizes):
    ways, span = sizes[number], math.prod(sizes[:number])
    own = lax.axis_index("cell") // span % ways
    return [lax.rem(own + s, ways) for s in range(ways)]


def begin_kernel(wide, left_ref, right_ref, out_ref):
    extra = left_ref.shape[0] - out_ref.shape[0]
    left = left_ref[extra:, :]
    for n in range(right_ref.shape[0] // wide):
        here = slice(n * wide, (n + 1) * wide)
        out_ref[:, here] = lax.dot_general(
            left, right_ref[here, :], (((1,), (1,)), ((), ())), preferred_element_type=F32
        )


def begin(left, right, rows):
    columns = right.shape[0]
    return pl.pallas_call(
        functools.partial(begin_kernel, min(columns, 256)),
        in_specs=[whole()] * 2,
        out_specs=whole(),
        out_shape=jax.ShapeDtypeStruct((rows, columns), F32),
        compiler_params=params(8),
        cost_estimate=SHORT,
        name="begin",
    )(left, right)


def contract_kernel(sizes, wide, count, begun, pieces, *refs):
    left_refs, right_refs = refs[:count], refs[count : 2 * count]
    outs, scratch = refs[2 * count + begun : -1], refs[-1]
    columns = right_refs[0].shape[0]
    places = digits(0, sizes)
    left = jnp.concatenate([ref[...] for ref in left_refs], axis=1)
    for n in range(columns // wide):
        here = slice(n * wide, (n + 1) * wide)
        right = jnp.concatenate([ref[here, :] for ref in right_refs], axis=1)
        value = lax.dot_general(left, right, (((1,), (1,)), ((), ())), preferred_element_type=F32)
        if begun:
            value = value + refs[2 * count][:, here]
        scratch[n % 2] = value.reshape(scratch.shape[1:])
        for q in range(outs[0].shape[0]):
            outs[0][q, :, here] = scratch[n % 2, q * sizes[0] + places[0]]
            for s, place in enumerate(places[1:]):
                piece, at = divmod(n * wide, columns // pieces)
                out = outs[1 + s * pieces + piece]
                out[q, :, at : at + wide] = scratch[n % 2, q * sizes[0] + place].astype(BF16)


def contract(left, right, sizes, pieces=1, begun=()):
    columns = right[0].shape[0]
    rows = left[0].shape[0]
    owners = math.prod(sizes)
    wide = min(columns, 256)
    pieces = pieces if columns // wide % pieces == 0 else 1
    shape = (owners // sizes[0], rows // owners, columns)
    part = (*shape[:2], columns // pieces)
    kept, *sent = pl.pallas_call(
        functools.partial(contract_kernel, sizes, wide, len(left), len(begun), pieces),
        in_specs=[whole()] * (2 * len(left) + len(begun)),
        out_specs=[whole()] * (1 + (sizes[0] - 1) * pieces),
        out_shape=[jax.ShapeDtypeStruct(shape, F32)]
        + [jax.ShapeDtypeStruct(part, BF16)] * ((sizes[0] - 1) * pieces),
        scratch_shapes=[pltpu.VMEM((2, owners, rows // owners, wide), F32)],
        compiler_params=params(8),
        cost_estimate=SHORT,
        name="contract",
    )(*left, *right, *begun)
    return [kept] + [sent[s * pieces : (s + 1) * pieces] for s in range(sizes[0] - 1)]


def fold_kernel(number, sizes, counts, *refs):
    kept_ref, arrived_refs, outs = refs[0], iter(refs[1 : 1 + sum(counts)]), refs[1 + sum(counts) :]
    arrived = [[next(arrived_refs) for _ in range(count)] for count in counts]
    places = [0] if number == len(sizes) else digits(number, sizes)
    ways = len(places)
    for q in range(kept_ref.shape[0] // ways):
        for out, place in zip(outs, places):
            total = kept_ref[q * ways + place]
            for pieces in arrived:
                values = [ref[q * ways + place].astype(F32) for ref in pieces]
                total = total + jnp.concatenate(values, axis=-1)
            out[q] = total.astype(out.dtype)


def fold(kept, arrived, number, sizes, all_leave=False):
    ways = 1 if number == len(sizes) else sizes[number]
    shape = (kept.shape[0] // ways, *kept.shape[1:])
    return pl.pallas_call(
        functools.partial(fold_kernel, number, sizes, [len(pieces) for pieces in arrived]),
        in_specs=[whole()] * (1 + sum(len(pieces) for pieces in arrived)),
        out_specs=[whole()] * ways,
        out_shape=[jax.ShapeDtypeStruct(shape, BF16 if s or all_leave else F32) for s in range(ways)],
        compiler_params=params(8),
        cost_estimate=SHORT,
        name="fold",
    )(kept, *[piece for pieces in arrived for piece in pieces])


def shifted(block, axis, distance, size, span, turn=0):
    reach, turns = lax.axis_size(axis), lax.axis_size("mode") if turn else 1
    route = []
    for i in range(reach):
        digit = i // span % size
        to = i + ((digit + distance) % size - digit) * span
        route += [(i * turns + m, to * turns + (m + turn) % turns) for m in range(turns)]
    return lax.ppermute(block, (axis, "mode") if turn else axis, route)


def stages(count):
    sizes = []
    while count % 4 == 0 and count > 4:
        sizes, count = sizes + [4], count // 4
    if count == 4:
        sizes, count = sizes + [2], 2
    return [count] + sizes[::-1] if count > 1 else sizes[::-1]


def stage(parts, number, sizes, all_leave=False):
    span = math.prod(sizes[:number])
    arrived = []
    for s, part in enumerate(parts[1:]):
        pieces = part if isinstance(part, list) else [part]
        arrived.append([shifted(piece, "cell", s + 1, sizes[number], span) for piece in pieces])
    return fold(parts[0], arrived, number + 1, sizes, all_leave)


def columns_of(flat, first, blocks, total, found, adv, mode, me, advect_count, per_block):
    rows, groups = found.shape[0], flat.shape[2] // LANES
    part = lax.rem(mode // per_block - me + total, total)
    slot = (part * advect_count + adv) * per_block + lax.rem(mode, per_block)
    lane = jnp.broadcast_to(lax.rem(slot, LANES), (rows, LANES))
    group = jnp.broadcast_to(slot // LANES, (rows, LANES))
    for b in range(blocks):
        for s in range(groups):
            source = flat[b, :, s * LANES : (s + 1) * LANES]
            taken = jnp.take_along_axis(source, lane, axis=1)
            found = jnp.where(group == (first + b) * groups + s, taken, found)
    return found


def prepare_kernel(blocks, advect_count, per_block, scale_factor, adv_ref, mode_ref, own_ref, amp_ref, high_ref, low_ref, found_ref, flat, amps, sems):
    steps, tall, _ = amps.shape
    copies = []
    for i in range(steps):
        copies.append(pltpu.make_async_copy(amp_ref.at[pl.ds(i * tall, tall)], amps.at[i], sems.at[i]))
        copies[-1].start()
    flat[0] = own_ref[0] * scale_factor
    for g in range(found_ref.shape[1] // LANES):
        here = slice(g * LANES, (g + 1) * LANES)
        found = jnp.zeros((found_ref.shape[0], LANES), F32)
        me = lax.axis_index("mode")
        pairs = adv_ref[:, here], mode_ref[:, here]
        found_ref[:, here] = columns_of(flat, 0, 1, blocks, found, *pairs, me, advect_count, per_block)
    for i in range(steps):
        copies[i].wait()
        amp = amps[i]
        high = amp.astype(BF16)
        high_ref[i * tall : (i + 1) * tall, :] = high
        low_ref[i * tall : (i + 1) * tall, :] = (amp - high.astype(F32)).astype(BF16)


def prepare(pair_adv, pair_mode, own, amp, blocks, advect_count, scale_factor):
    pairs, snaps = amp.shape
    _, rows, columns = own.shape
    tall = 256 if pairs % 256 == 0 else pairs
    per_block = columns // advect_count
    return pl.pallas_call(
        functools.partial(prepare_kernel, blocks, advect_count, per_block, scale_factor),
        in_specs=[whole()] * 3 + [whole(pltpu.HBM)],
        out_specs=[whole()] * 3,
        out_shape=[jax.ShapeDtypeStruct(amp.shape, BF16)] * 2 + [jax.ShapeDtypeStruct((rows, pairs), F32)],
        scratch_shapes=[
            pltpu.VMEM((1, rows, columns), F32),
            pltpu.VMEM((pairs // tall, tall, snaps), F32),
            pltpu.SemaphoreType.DMA((pairs // tall,)),
        ],
        compiler_params=params(24),
        cost_estimate=pl.CostEstimate(flops=4 * amp.size, bytes_accessed=8 * amp.size, transcendentals=0),
        name="prepare",
    )(pair_adv.reshape(1, pairs), pair_mode.reshape(1, pairs), own, amp)


def finish_kernel(advect_count, per_block, scale_factor, counts, adv_ref, mode_ref, *refs):
    *part_refs, high_ref, low_ref, found_ref, tensor_ref, out_ref, flat = refs
    blocks, rows = flat.shape[0], flat.shape[1]
    me = lax.axis_index("mode")
    tall = 512 if high_ref.shape[0] % 512 == 0 else high_ref.shape[0]
    steps = high_ref.shape[0] // tall
    terms = iter(part_refs)
    for s, count in enumerate(counts):
        total = next(terms)[0].astype(F32)
        for _ in range(count - 1):
            total = total + next(terms)[0].astype(F32)
        flat[s] = total * scale_factor
    for b in range(blocks):
        for j in range(advect_count):
            at = slice(j * per_block, (j + 1) * per_block)
            value = flat[0, :, at]
            for s in range(1, blocks):
                value = jnp.where(lax.rem(me + s, blocks) == b, flat[s, :, at], value)
            tensor_ref[:, j, b * per_block : (b + 1) * per_block] = value

    def columns(i):
        high, low = [], []
        for g in range(i * tall // LANES, (i + 1) * tall // LANES):
            here = slice(g * LANES, (g + 1) * LANES)
            pairs = adv_ref[:, here], mode_ref[:, here]
            found = columns_of(
                flat.at[1:], 1, blocks - 1, blocks, found_ref[:, here], *pairs, me, advect_count, per_block
            )
            high.append(found.astype(BF16).astype(F32))
            low.append(found - high[-1])
        both = [jnp.concatenate(high, axis=1), jnp.concatenate(low, axis=1)]
        return jnp.concatenate(both, axis=0).astype(BF16)

    total = jnp.zeros(out_ref.shape, F32)
    now = columns(0)
    for i in range(steps):
        here = slice(i * tall, (i + 1) * tall)
        term = jnp.dot(now, high_ref[here, :], preferred_element_type=F32)
        small = jnp.dot(now[:rows], low_ref[here, :], preferred_element_type=F32)
        if i < steps - 1:
            now = columns(i + 1)
        total = total + (term[:rows] + (term[rows:] + small))
    out_ref[...] = total


def finish(pair_adv, pair_mode, parts, high, low, found, advect_count, scale_factor):
    pairs, snaps = high.shape
    _, rows, columns = parts[0][0].shape
    blocks = len(parts)
    counts = [len(part) for part in parts]
    terms = [term for part in parts for term in part]
    per_block = columns // advect_count
    return pl.pallas_call(
        functools.partial(finish_kernel, advect_count, per_block, scale_factor, counts),
        in_specs=[whole()] * (5 + len(terms)),
        out_specs=[whole(), whole()],
        out_shape=[
            jax.ShapeDtypeStruct((rows, advect_count, blocks * per_block), F32),
            jax.ShapeDtypeStruct((rows, snaps), F32),
        ],
        scratch_shapes=[pltpu.VMEM((blocks, rows, columns), F32)],
        compiler_params=params(8),
        cost_estimate=SHORT,
        name="finish",
    )(pair_adv.reshape(1, pairs), pair_mode.reshape(1, pairs), *terms, high, low, found)


def shards(pod_modes, slab_map, slab_volume, advect_index, pair_adv, pair_mode, pair_amp):
    comps, mode_block, planes, rows_y, width = pod_modes.shape
    mode_devs = lax.axis_size("mode")
    cell_devs = lax.axis_size("cell")
    advect_count = advect_index.shape[0]
    scale_factor = float(planes * rows_y * cell_devs * width) ** (-0.5)
    me = lax.axis_index("mode")
    rows_here = mode_block // cell_devs

    flat = pod_modes.reshape(comps, mode_block, planes * rows_y, width)
    first, held = lead(flat, advect_index, planes, rows_y, rows_y - 1)
    rows, before = {}, first
    for r in [rows_y - 1, *range(rows_y - 1)]:
        rows[r] = edge(held, before, planes, rows_y, r)
        before = rows[r]
    weight = weights(slab_map, slab_volume, before)
    own = [rows[r] for r in range(rows_y)]
    ahead = [shifted(first, "mode", s, mode_devs, 1) for s in range(1, mode_devs)]
    arrived = [[shifted(block, "mode", s, mode_devs, 1) for block in own[:-1]] for s in range(1, mode_devs)]
    up = [(i, i + 1) for i in range(cell_devs - 1)]
    rows[-1] = lax.ppermute(rows[rows_y - 1], "cell", up)
    rows[rows_y] = lax.ppermute(rows[0], "cell", [(j, i) for i, j in up])
    leads = [first] + ahead
    right = []
    for r in range(rows_y):
        if right:
            right[-1], rows[r + 1] = lax.optimization_barrier((right[-1], rows[r + 1]))
        block = advected(leads, rows[r], rows[r - 1], rows[r + 1], weight, rows_y, r, advect_count)
        right.append(block.reshape(-1, block.shape[-1]))

    sizes = stages(cell_devs)
    early, last = min(1, len(sizes)), len(sizes) - 1

    def summed(parts, first, end, sizes):
        for number in range(first, min(end, len(sizes))):
            parts = stage(parts, number, sizes)
        return list(parts)

    pairwise = sizes[:-1] + [2, 2] if sizes[-1] == 4 else sizes
    mine = contract(own, right, pairwise)
    mine[0], ahead = lax.optimization_barrier((mine[0], ahead))
    begun = begin(ahead[0], right[-1], mode_block)
    mine = summed(mine, 0, early, pairwise)
    mine[0], arrived = lax.optimization_barrier((mine[0], arrived))
    mine = summed(mine, early, early + 1, pairwise)
    result = []
    for s in range(1, mode_devs):
        begun = begun if s == 1 else begin(ahead[s - 1], right[-1], mode_block)
        block = contract(arrived[s - 1], right[:-1], sizes, 4, [begun])
        block = summed(block, 0, early, sizes)
        if s == 1:
            mine, block = lax.optimization_barrier((mine, block))
        block = stage(summed(block, early, last - 1, sizes), last - 1, sizes, True)
        if s == 1:
            mine = summed(mine, early + 1, early + 2, pairwise)
            mine = summed(mine, early + 2, len(pairwise), pairwise)
            block, pair_amp = lax.optimization_barrier((block, pair_amp))
            mine, pair_amp = lax.optimization_barrier((mine, pair_amp))
            result.append(mine)
        span = math.prod(sizes[:last])
        result.append([shifted(b, "cell", n, sizes[last], span, mode_devs - s) for n, b in enumerate(block)])
    high, low, found = prepare(
        pair_adv, pair_mode, result[0][0], pair_amp, mode_devs, advect_count, scale_factor
    )
    tensor, response = finish(pair_adv, pair_mode, result, high, low, found, advect_count, scale_factor)
    return (tensor, response)


def solution(mesh):
    in_specs = (P(None, "mode", None, "cell", None), P(None, "cell", None), P(), P(), P(), P(), P())
    out_specs = (P(("mode", "cell"), None, None), P(("mode", "cell"), None))
    return jax.shard_map(shards, mesh=mesh, in_specs=in_specs, out_specs=out_specs, check_vma=False)
```
